256 devices in a mesh: rows: 32 (over z, x), dp: 8 (over y, core).
Axes of the slice: x: 4, y: 4, z: 8, core: 2. Of those that a mesh axis runs over, the one named last changes fastest.
Arguments:
- pixels: bfloat16 [8, 2048, 8, 768], P('dp', 'rows'), may hold values from -6 to 6
- kernel_two: float32 [49, 768], replicated, may hold values from -0.875 to 0.875
- bias_two: float32 [768], replicated, may hold values from -3 to 3
- gain_two: float32 [768], replicated, may hold values from 0.4 to 1.6
- down_weight: bfloat16 [3072, 1536], P(('rows', 'dp')), may hold values from -0.109375 to 0.109375
- down_bias: float32 [1536], replicated, may hold values from -3 to 3
- kernel_three: float32 [49, 1536], replicated, may hold values from -0.875 to 0.875
- bias_three: float32 [1536], replicated, may hold values from -3 to 3
- cotangent: bfloat16 [8, 2048, 4, 1536], P('dp', 'rows'), may hold values from -6 to 6
- tile_height: int32 [8, 512], P('dp'), may hold values from 1 to 4, as said below
- tile_width: int32 [8, 512], P('dp'), may hold values from 2 to 8, as said below
- tile_owner: int32 [8, 512], P('dp'), may hold values from 0 to 31, as said below
Outputs:
- features: bfloat16 [8, 2048, 4, 1536], P('dp', 'rows')
- pixel_grad: bfloat16 [8, 2048, 8, 768], P('dp', 'rows')
- kernel_two_grad: float32 [49, 768], replicated
- bias_two_grad: float32 [768], replicated
- gain_two_grad: float32 [768], replicated
- kernel_three_grad: float32 [49, 1536], replicated
- bias_three_grad: float32 [1536], replicated
The draws below stay inside these ranges and needn't reach their ends.
Inputs may be any that keep to these rules, and one draw needn't show every extreme that they name: `tile_owner`: owners come in a cycle of 32 tiles repeated along the strip: every owner once a cycle, in one order for all cycles of a group. `tile_height`: heights follow a class that depends only on the place in the cycle: the first tile of a cycle is of class 2, the next 8 of class 4, the rest hold 7 tiles of class 2 and 16 of class 1 in some order; every tile has its class's height except the strip's first tile, which has 1 row fewer, and its last tile, which has 1 row more. The heights of a group sum to 1024. One device's section-3 rows go to one owner at most 4 at a time and an owner holds at most 64 rows; both bounds are reached. `tile_width`: widths are even.
All inputs are finite; a program needn't handle non-finite values.
Results may differ from the reference program's by a relative error of at most 0.011.
Values may be sent and summed in bfloat16 or wider, within the bound.
A program may use at most 192 MiB of HBM per device.

```python
import math
import jax
import jax.numpy as jnp
from jax import lax

C2 = 768
C3 = 1536
TAPS = 49
W2 = 8
R3_DEV = 32
W3 = 4
KD = 3072
OWNCAP = 64
NTILES = 512
ROWS2 = 2048
GROUPS = 8
PIX_ALL = 131072
N_ROWS = 32


def tile_plan(key):
    group_keys = jax.random.split(key, GROUPS)

    def one_group(group_key):
        order_key, class_key = jax.random.split(group_key)
        holders = jax.random.permutation(order_key, N_ROWS).astype(jnp.int32)
        tail_len = N_ROWS - 1 - N_ROWS // 4
        tail_part = jnp.where(jnp.arange(tail_len) < N_ROWS // 4 - 1, 2, 1).astype(jnp.int32)
        tail_part = jax.random.permutation(class_key, tail_part)
        classes = jnp.concatenate([jnp.full((1,), 2, jnp.int32), jnp.full((N_ROWS // 4,), 4, jnp.int32), tail_part])
        return (holders, classes * (R3_DEV // N_ROWS))
    holders, heights = jax.vmap(one_group)(group_keys)
    owners = jnp.tile(holders, (1, N_ROWS // 2)).astype(jnp.int32)
    heights = jnp.tile(heights, (1, N_ROWS // 2)).astype(jnp.int32)
    column = jnp.arange(NTILES)[None, :]
    unit = R3_DEV // N_ROWS
    heights = heights - jnp.where(column == 0, unit, 0) + jnp.where(column == NTILES - 1, unit, 0)
    return (owners, heights.astype(jnp.int32))


def draw_tile_height(key, part):
    return tile_plan(key)[1]


def draw_tile_owner(key, part):
    return tile_plan(key)[0]


def draw_tile_width(key, part):
    key = jax.random.fold_in(key, 5)
    widths = 2 * jax.random.randint(key, (GROUPS, NTILES), 1, W2 // 2 + 1)
    column = jnp.arange(NTILES)[None, :]
    return jnp.where(column == 0, W2, widths).astype(jnp.int32)


def steps_of(rng, shape, shards, low, largest):
    def one(position, shards_of):
        steps = jax.random.uniform(jax.random.fold_in(jax.random.fold_in(rng, 6), position), (shards_of,), jnp.float32, low / len(shards), largest / len(shards))
        return jnp.repeat(jnp.exp(steps), shape[position] // shards_of).reshape((-1,) + (1,) * (len(shape) - position - 1))

    level = one(*shards[0])
    for cut in shards[1:]:
        level = level * one(*cut)
    return level


def normal_values(own_key, dims, deviation, most, cuts=(), kind=jnp.bfloat16):
    entries = deviation * jax.random.normal(own_key, dims, jnp.float32)
    if cuts:
        entries = entries * steps_of(own_key, dims, cuts, -0.22, 0.18)
    return jnp.clip(entries, -most, most).astype(kind)


def setup_inputs(seed: int = 0) -> dict:
    keys = jax.random.split(jax.random.key(seed), 13)
    pixels = normal_values(keys[0], (GROUPS, ROWS2, W2, C2), 1.0, 6.0, ((0, 8), (1, 32)))
    kernel_two = normal_values(keys[1], (TAPS, C2), TAPS ** -0.5, 0.875, (), jnp.float32)
    bias_two = normal_values(keys[2], (C2,), 0.5, 3.0, (), jnp.float32)
    gain_two = jnp.clip(1.0 + 0.12 * jax.random.normal(keys[3], (C2,), jnp.float32), 0.4, 1.6)
    down_weight = normal_values(keys[4], (KD, C3), KD ** -0.5, 0.109375, ((0, 256),))
    down_bias = normal_values(keys[5], (C3,), 0.5, 3.0, (), jnp.float32)
    kernel_three = normal_values(keys[6], (TAPS, C3), TAPS ** -0.5, 0.875, (), jnp.float32)
    bias_three = normal_values(keys[7], (C3,), 0.5, 3.0, (), jnp.float32)
    cotangent = normal_values(keys[8], (GROUPS, N_ROWS * OWNCAP, W3, C3), 1.0, 6.0, ((0, 8), (1, 32)))
    tile_height = draw_tile_height(jax.random.fold_in(keys[12], 71), 0)
    tile_width = draw_tile_width(jax.random.fold_in(keys[12], 71), 0)
    tile_owner = draw_tile_owner(jax.random.fold_in(keys[12], 71), 0)
    return {"pixels": pixels, "kernel_two": kernel_two, "bias_two": bias_two, "gain_two": gain_two, "down_weight": down_weight, "down_bias": down_bias, "kernel_three": kernel_three, "bias_three": bias_three, "cotangent": cotangent, "tile_height": tile_height, "tile_width": tile_width, "tile_owner": tile_owner}


epsilon = 1e-06

def table_pick(table, index):
    matches = index[..., None] == jnp.arange(table.shape[0], dtype=jnp.int32)
    return lax.optimization_barrier(jnp.sum(jnp.where(matches, table, 0), axis=-1)).astype(jnp.int32)

def tile_tables(heights, owners):
    ends_at = jnp.cumsum(heights).astype(jnp.int32)
    starts_at = (ends_at - heights).astype(jnp.int32)
    order = jnp.arange(heights.shape[0], dtype=jnp.int32)
    earlier = (owners[:, None] == owners[None, :]) & (order[None, :] < order[:, None])
    own_start = lax.optimization_barrier(jnp.sum(jnp.where(earlier, heights[None, :], 0), axis=1)).astype(jnp.int32)
    return (starts_at, ends_at, own_start)

def tile_of(rows_at, starts_at, total):
    inside = lax.optimization_barrier(jnp.sum((starts_at[None, :] <= rows_at[:, None]).astype(jnp.int32), axis=1)).astype(jnp.int32) - 1
    return jnp.where((rows_at >= 0) & (rows_at < total), inside, -1).astype(jnp.int32)

def take_rows(source, index, valid):
    picked = jnp.take(source, jnp.clip(index, 0, source.shape[0] - 1).astype(jnp.int32), axis=0)
    return jnp.where(valid[:, None, None], picked, jnp.zeros((), source.dtype))

def depthwise(field, kernel, tiles_pad):
    length = field.shape[0] - 6
    width = field.shape[1]
    padded = jnp.pad(field, ((0, 0), (3, 3), (0, 0)))
    total = jnp.zeros((length, width, field.shape[2]), jnp.float32)
    for row_off in range(7):
        same = tiles_pad[row_off:row_off + length] == tiles_pad[3:3 + length]
        block = jnp.where(same[:, None, None], padded[row_off:row_off + length], 0.0)
        for col_off in range(7):
            total = total + block[:, col_off:col_off + width] * kernel[row_off * 7 + col_off]
    return total

def depthwise_back(grads, kernel, tiles_pad):
    length = grads.shape[0] - 6
    width = grads.shape[1]
    padded = jnp.pad(grads, ((0, 0), (3, 3), (0, 0)))
    total = jnp.zeros((length, width, grads.shape[2]), jnp.float32)
    for row_off in range(7):
        first = 6 - row_off
        same = tiles_pad[first:first + length] == tiles_pad[3:3 + length]
        block = jnp.where(same[:, None, None], padded[first:first + length], 0.0)
        for col_off in range(7):
            total = total + block[:, 6 - col_off:6 - col_off + width] * kernel[row_off * 7 + col_off]
    return total

def kernel_terms(grads, field, tiles_pad):
    length = grads.shape[0]
    width = grads.shape[1]
    padded = jnp.pad(field, ((0, 0), (3, 3), (0, 0)))
    terms = []
    for row_off in range(7):
        same = tiles_pad[row_off:row_off + length] == tiles_pad[3:3 + length]
        block = jnp.where(same[:, None, None], padded[row_off:row_off + length], 0.0)
        for col_off in range(7):
            terms.append(lax.optimization_barrier(jnp.sum(block[:, col_off:col_off + width] * grads, axis=(0, 1))))
    return jnp.stack(terms)

def reference(pixels, kernel_two, bias_two, gain_two, down_weight, down_bias, kernel_three, bias_three, cotangent, tile_height, tile_width, tile_owner):
    total = N_ROWS * R3_DEV
    strip = 2 * total
    negative = jnp.full((3,), -1, jnp.int32)

    def group(items):
        pixels_one, grad_one, heights, widths, owners = items
        starts_at, ends_at, own_start = tile_tables(heights, owners)
        rows_two = jnp.arange(strip + 6, dtype=jnp.int32) - 3
        tiles_two = tile_of(jnp.floor_divide(rows_two, 2), starts_at, total)
        cols_two = jnp.arange(W2, dtype=jnp.int32)[None, :] < table_pick(widths, tiles_two)[:, None]
        field = jnp.pad(pixels_one.astype(jnp.float32), ((3, 3), (0, 0), (0, 0)))
        masked = jnp.where(cols_two[:, :, None], field, 0.0)
        inner = cols_two[3:3 + strip]
        act = jnp.where(inner[:, :, None], depthwise(masked, kernel_two, tiles_two) + bias_two, 0.0)
        centred = act - lax.optimization_barrier(jnp.mean(act, axis=-1, keepdims=True))
        inverse = lax.rsqrt(lax.optimization_barrier(jnp.mean(centred * centred, axis=-1, keepdims=True)) + epsilon)
        nhat = centred * inverse
        normed = (nhat * gain_two).astype(jnp.bfloat16)
        patches = normed.reshape(total, 2, W3, 2, C2).transpose(0, 2, 1, 3, 4).reshape(total * W3, KD)
        tiles_three = tile_of(jnp.arange(total, dtype=jnp.int32), starts_at, total)
        cols_three = jnp.arange(W3, dtype=jnp.int32)[None, :] < (table_pick(widths, tiles_three) // 2)[:, None]
        projected = jnp.dot(patches, down_weight, preferred_element_type=jnp.float32).reshape(total, W3, C3)
        down = jnp.where(cols_three[:, :, None], projected + down_bias, 0.0).astype(jnp.bfloat16)
        pad_three = jnp.concatenate([negative, tiles_three, negative])
        down_field = jnp.pad(down.astype(jnp.float32), ((3, 3), (0, 0), (0, 0)))
        extra = jnp.where(cols_three[:, :, None], depthwise(down_field, kernel_three, pad_three) + bias_three, 0.0)
        features = (down.astype(jnp.float32) + extra).astype(jnp.bfloat16)
        holder = jnp.repeat(jnp.arange(N_ROWS, dtype=jnp.int32), OWNCAP)
        slot = jnp.tile(jnp.arange(OWNCAP, dtype=jnp.int32), N_ROWS)
        hits = (owners[None, :] == holder[:, None]) & (own_start[None, :] <= slot[:, None]) & (slot[:, None] < own_start[None, :] + heights[None, :])
        present = jnp.any(hits, axis=1)
        tile_id = lax.optimization_barrier(jnp.sum(jnp.where(hits, jnp.arange(NTILES, dtype=jnp.int32)[None, :], 0), axis=1)).astype(jnp.int32)
        rows_at = table_pick(starts_at, tile_id) + slot - table_pick(own_start, tile_id)
        features_own = take_rows(features, rows_at, present)
        strip_index = table_pick(owners, tiles_three) * OWNCAP + table_pick(own_start, tiles_three) + jnp.arange(total, dtype=jnp.int32) - table_pick(starts_at, tiles_three)
        grad_strip = jnp.take(grad_one, strip_index.astype(jnp.int32), axis=0)
        grad_out = jnp.where(cols_three[:, :, None], grad_strip.astype(jnp.float32), 0.0)
        grad_field = jnp.pad(grad_out, ((3, 3), (0, 0), (0, 0)))
        grad_down = jnp.where(cols_three[:, :, None], grad_out + depthwise_back(grad_field, kernel_three, pad_three), 0.0).astype(jnp.bfloat16)
        kernel_three_part = kernel_terms(grad_out, down_field, pad_three)
        bias_three_part = lax.optimization_barrier(jnp.sum(grad_out, axis=(0, 1)))
        grad_patch = lax.dot_general(grad_down.reshape(total * W3, C3), down_weight, (((1,), (1,)), ((), ())), preferred_element_type=jnp.float32).astype(jnp.bfloat16)
        grad_normed = grad_patch.reshape(total, W3, 2, 2, C2).transpose(0, 2, 1, 3, 4).reshape(strip, W2, C2).astype(jnp.float32)
        gain_part = lax.optimization_barrier(jnp.sum(grad_normed * nhat, axis=(0, 1)))
        scaled = grad_normed * gain_two
        grad_act = inverse * (scaled - lax.optimization_barrier(jnp.mean(scaled, axis=-1, keepdims=True)) - nhat * lax.optimization_barrier(jnp.mean(scaled * nhat, axis=-1, keepdims=True)))
        grad_act = jnp.where(inner[:, :, None], grad_act, 0.0).astype(jnp.bfloat16)
        act_field = jnp.pad(grad_act.astype(jnp.float32), ((3, 3), (0, 0), (0, 0)))
        pixel_grad = jnp.where(inner[:, :, None], depthwise_back(act_field, kernel_two, tiles_two), 0.0).astype(jnp.bfloat16)
        kernel_two_part = kernel_terms(grad_act.astype(jnp.float32), masked, tiles_two)
        bias_two_part = lax.optimization_barrier(jnp.sum(grad_act.astype(jnp.float32), axis=(0, 1)))
        return (features_own, pixel_grad, (kernel_two_part, bias_two_part, gain_part, kernel_three_part, bias_three_part))
    features, pixel_grad, parts = lax.map(group, (pixels, cotangent, tile_height, tile_width, tile_owner))
    factor = 1.0 / math.sqrt(PIX_ALL)
    sums = [lax.optimization_barrier(jnp.sum(part, axis=0)) * factor for part in parts]
    return (features, pixel_grad, sums[0], sums[1], sums[2], sums[3], sums[4])
```

```python
import functools
import math
from types import SimpleNamespace

import jax
import jax.numpy as jnp
from jax import lax
from jax.experimental import pallas as pl
from jax.experimental.pallas import tpu as pltpu
from jax.sharding import PartitionSpec as P

MESH = pl.DeviceIdType.MESH
F32 = jnp.float32
BF16 = jnp.bfloat16
epsilon = 1e-06

NZ, NX, NY = 8, 4, 4
NROWS = NZ * NX
NDP = 2 * NY
SIZE = {"x": NX, "y": NY, "z": NZ}
ORDERS = (("x", "y", "z"), ("y", "z", "x"), ("z", "x", "y"))
WIN = 56
OWN = 12
BASE = 8


def spread_taps(r):
    def one(t, _):
        row = r.k2[pl.ds(t, 1), :]
        for ch in range(6):
            r.kb2[ch, t] = jnp.broadcast_to(row[:, ch * 128 : ch * 128 + 128], (8, 128))
        row = r.k3[pl.ds(t, 1), :]
        for ch in range(12):
            r.kb3[ch, t] = jnp.broadcast_to(row[:, ch * 128 : ch * 128 + 128], (8, 128))
        return 0

    lax.fori_loop(0, 49, one, 0)
    for ch in range(6):
        r.kb2[ch, 49] = jnp.broadcast_to(r.b2[:, ch * 128 : ch * 128 + 128], (8, 128))
    for ch in range(12):
        r.kb3[ch, 49] = jnp.broadcast_to(r.b3[:, ch * 128 : ch * 128 + 128], (8, 128))


def load_pixels(r):
    def one(ac, _):
        inside = r.masks[7 + (ac % 8) // 2]
        for ch in range(6):
            r.x[ch, ac] = r.xin[ac, :, ch * 128 : ch * 128 + 128].astype(F32) * inside
        return 0

    lax.fori_loop(0, 16, one, 0)


def conv2(r, src, ch, a, s0, flip, accs):
    for i in range(7):
        t = a + i - 3
        par, shift = t % 2, t // 2
        cols = [src[ch, par * 8 + c, pl.ds(s0 + shift, 8), :] for c in range(8)]
        if shift != 0:
            same = r.masks[shift + 3, pl.ds(s0, 8), :]
            cols = [v * same for v in cols]
        for j in range(7):
            tap = 7 * i + j
            k = r.kb2[ch, 48 - tap if flip else tap]
            for c in range(8):
                if 0 <= c + j - 3 < 8:
                    term = cols[c + j - 3] * k
                    accs[c] = term if accs[c] is None else accs[c] + term
    return accs


def conv3(r, src, ch, s0, flip, accs):
    for i in range(7):
        cols = [src[ch, q, pl.ds(s0 + i - 3, 8), :] for q in range(4)]
        if i != 3:
            same = r.masks[i, pl.ds(s0, 8), :]
            cols = [v * same for v in cols]
        for j in range(7):
            tap = 7 * i + j
            k = r.kb3[ch, 48 - tap if flip else tap]
            for q in range(4):
                if 0 <= q + j - 3 < 4:
                    term = cols[q + j - 3] * k
                    accs[q] = term if accs[q] is None else accs[q] + term
    return accs


def forward_two(r, ch):
    def block(b, _):
        s0 = BASE + 8 * b
        for a in range(2):
            accs = conv2(r, r.x, ch, a, s0, False, [r.kb2[ch, 49]] * 8)
            for c in range(8):
                r.act[ch, a * 8 + c, pl.ds(8 * b, 8), :] = accs[c]
        return 0

    lax.fori_loop(0, 5, block, 0)


def channel_mean(parts):
    total = parts[0]
    for v in parts[1:]:
        total = total + v
    return jnp.sum(total, axis=1, keepdims=True) * (1.0 / 768)


def norm_two(r):
    def one(ac, _):
        a, col = ac // 8, ac % 8
        q, b2 = col // 2, col % 2
        for b in range(5):
            inside = r.masks[7 + q, pl.ds(BASE + 8 * b, 8), :]
            act = [r.act[ch, ac, 8 * b : 8 * b + 8, :] * inside for ch in range(6)]
            mean = channel_mean(act)
            act = [v - mean for v in act]
            inverse = lax.rsqrt(channel_mean([v * v for v in act]) + epsilon)
            r.inv[ac, 8 * b : 8 * b + 8, :] = jnp.broadcast_to(inverse, (8, 128))
            for ch in range(6):
                nhat = act[ch] * inverse
                r.act[ch, ac, 8 * b : 8 * b + 8, :] = nhat
                gain = r.gain[:, ch * 128 : ch * 128 + 128]
                r.lhs[a * 2 + b2, pl.ds(q * 40 + 8 * b, 8), ch * 128 : ch * 128 + 128] = nhat * gain
        return 0

    lax.fori_loop(0, 16, one, 0)


def weight_panel(r, n, ab):
    return r.w[n // 2, n % 2, pl.ds(2 * ab, 2)].reshape(768, 384)


def project(r, n):
    total = jnp.zeros((160, 384), F32)
    for ab in range(4):
        total = total + jnp.dot(
            r.lhs[ab].astype(BF16), weight_panel(r, n, ab), preferred_element_type=F32
        )
    for cb in range(3):
        ch = n * 3 + cb
        bias = r.db[:, ch * 128 : ch * 128 + 128]
        for q in range(4):
            part = total[q * 40 : q * 40 + 40, cb * 128 : cb * 128 + 128] + bias
            part = part * r.masks[7 + q, BASE : BASE + 40, :]
            r.down[ch, q, BASE : BASE + 40, :] = part.astype(BF16).astype(F32)


def forward_three(r):
    def one(ch, _):
        for b in range(4):
            s0 = OWN + 8 * b
            accs = conv3(r, r.down, ch, s0, False, [r.kb3[ch, 49]] * 4)
            for q in range(4):
                inside = r.masks[7 + q, s0 : s0 + 8, :]
                out = r.down[ch, q, s0 : s0 + 8, :] + accs[q] * inside
                r.feat[ch, q * 32 + 8 * b : q * 32 + 8 * b + 8, :] = out
        return 0

    lax.fori_loop(0, 12, one, 0)


def place_cotangent(r):
    for n in range(4):
        part = jnp.dot(
            r.pick_cot[...], r.cot_recv[:, n * 384 : n * 384 + 384], preferred_element_type=F32
        )
        for cb in range(3):
            for q in range(4):
                r.gout[n * 3 + cb, q] = part[q * WIN : q * WIN + WIN, cb * 128 : cb * 128 + 128]


def backward_three(r):
    def one(ch, _):
        for b in range(5):
            s0 = BASE + 8 * b
            accs = conv3(r, r.gout, ch, s0, True, [None] * 4)
            for q in range(4):
                inside = r.masks[7 + q, s0 : s0 + 8, :]
                out = (r.gout[ch, q, s0 : s0 + 8, :] + accs[q]) * inside
                r.gdown[ch, q * 40 + 8 * b : q * 40 + 8 * b + 8, :] = out
        return 0

    lax.fori_loop(0, 12, one, 0)


def row_sum(v):
    return jnp.sum(v, axis=0, keepdims=True)


def kernel_three(r):
    def one(ch, _):
        bias = None
        for i in range(7):
            accs = [None] * 7
            for b in range(4):
                s0 = OWN + 8 * b
                grads = [r.gout[ch, q, s0 : s0 + 8, :] for q in range(4)]
                if i == 0:
                    for v in grads:
                        bias = v if bias is None else bias + v
                if i != 3:
                    same = r.masks[i, s0 : s0 + 8, :]
                    grads = [v * same for v in grads]
                field = [r.down[ch, q, s0 + i - 3 : s0 + i + 5, :] for q in range(4)]
                for j in range(7):
                    for q in range(4):
                        if 0 <= q + j - 3 < 4:
                            term = grads[q] * field[q + j - 3]
                            accs[j] = term if accs[j] is None else accs[j] + term
            for j in range(7):
                r.sums[pl.ds((6 + ch) * 56 + 7 * i + j, 1), :] = row_sum(accs[j])
        r.sums[pl.ds((6 + ch) * 56 + 49, 1), :] = row_sum(bias)
        return 0

    lax.fori_loop(0, 12, one, 0)


def project_back(r, ab):
    total = jnp.zeros((160, 768), F32)
    for n in range(4):
        part = jnp.concatenate([r.gdown[n * 3 + cb].astype(BF16) for cb in range(3)], axis=1)
        total = total + lax.dot_general(
            part, weight_panel(r, n, ab), (((1,), (1,)), ((), ())), preferred_element_type=F32
        )
    r.lhs[ab] = total.astype(BF16).astype(F32)


def norm_back(r):
    zeros = jnp.zeros((8, 128), F32)

    def one(ac, carry):
        carry = list(carry)
        a, col = ac // 8, ac % 8
        q, b2 = col // 2, col % 2
        row = lax.broadcasted_iota(jnp.int32, (8, 128), 0)
        for b in range(5):
            inside = r.masks[7 + q, pl.ds(BASE + 8 * b, 8), :]
            inverse = r.inv[ac, 8 * b : 8 * b + 8, :] * inside
            nhat = [r.act[ch, ac, 8 * b : 8 * b + 8, :] for ch in range(6)]
            gn = [
                r.lhs[a * 2 + b2, pl.ds(q * 40 + 8 * b, 8), ch * 128 : ch * 128 + 128]
                for ch in range(6)
            ]
            scaled = [gn[ch] * r.gain[:, ch * 128 : ch * 128 + 128] for ch in range(6)]
            mean = channel_mean(scaled)
            mixed = channel_mean([s * v for s, v in zip(scaled, nhat)])
            for ch in range(6):
                grad = inverse * (scaled[ch] - mean - nhat[ch] * mixed)
                grad = grad.astype(BF16).astype(F32)
                r.gact[ch, ac, BASE + 8 * b : BASE + 8 * b + 8, :] = grad
                gain_term = gn[ch] * nhat[ch]
                if b in (0, 4):
                    keep = row >= 4 if b == 0 else row < 4
                    gain_term = jnp.where(keep, gain_term, 0.0)
                    grad = jnp.where(keep, grad, 0.0)
                carry[ch] = carry[ch] + grad
                carry[6 + ch] = carry[6 + ch] + gain_term
        return tuple(carry)

    sums = lax.fori_loop(0, 16, one, (zeros,) * 12)
    for ch in range(6):
        r.sums[ch * 56 + 49 : ch * 56 + 50, :] = row_sum(sums[ch])
        r.sums[ch * 56 + 50 : ch * 56 + 51, :] = row_sum(sums[6 + ch])


def kernel_two(r):
    def one(ch, _):
        for i in range(7):
            accs = [None] * 7
            for a in range(2):
                t = a + i - 3
                par, shift = t % 2, t // 2
                for b in range(4):
                    s0 = OWN + 8 * b
                    grads = [r.gact[ch, a * 8 + c, s0 : s0 + 8, :] for c in range(8)]
                    if shift != 0:
                        same = r.masks[shift + 3, s0 : s0 + 8, :]
                        grads = [v * same for v in grads]
                    field = [
                        r.x[ch, par * 8 + c, s0 + shift : s0 + shift + 8, :] for c in range(8)
                    ]
                    for j in range(7):
                        for c in range(8):
                            if 0 <= c + j - 3 < 8:
                                term = grads[c] * field[c + j - 3]
                                accs[j] = term if accs[j] is None else accs[j] + term
            for j in range(7):
                r.sums[pl.ds(ch * 56 + 7 * i + j, 1), :] = row_sum(accs[j])
        return 0

    lax.fori_loop(0, 6, one, 0)


def backward_two(r):
    def one(ch, _):
        for b in range(4):
            s0 = OWN + 8 * b
            for a in range(2):
                accs = conv2(r, r.gact, ch, a, s0, True, [None] * 8)
                for c in range(8):
                    inside = r.masks[7 + c // 2, s0 : s0 + 8, :]
                    r.pgrad[ch, a * 8 + c, 8 * b : 8 * b + 8, :] = accs[c] * inside
        return 0

    lax.fori_loop(0, 6, one, 0)
    for ch in range(6):
        r.pixel_grad[:, :, ch * 128 : ch * 128 + 128] = r.pgrad[ch].astype(BF16)


COMPUTE_SCRATCH = dict(
    kb2=((6, 50, 8, 128), F32),
    kb3=((12, 50, 8, 128), F32),
    x=((6, 16, WIN, 128), F32),
    act=((6, 16, 40, 128), F32),
    inv=((16, 40, 128), F32),
    lhs=((4, 160, 768), F32),
    down=((12, 4, WIN, 128), F32),
    feat=((12, 128, 128), F32),
    gout=((12, 4, WIN, 128), F32),
    gdown=((12, 160, 128), F32),
    gact=((6, 16, WIN, 128), F32),
    pgrad=((6, 16, 32, 128), F32),
)


class Comm:
    def __init__(self):
        rows, dp = lax.axis_index("rows"), lax.axis_index("dp")
        self.rows, self.dp = rows, dp
        self.pos = {"z": rows // NX, "x": rows % NX, "y": dp // 2}
        self.core = dp % 2

    def device(self, **moved):
        at = {**self.pos, "core": self.core, **moved}
        return (at["z"] * NX + at["x"], at["y"] * 2 + at["core"])

    def greet(self):
        barrier = pltpu.get_barrier_semaphore()

        def one(k, _):
            peer = (lax.rem(self.rows + k, NROWS), self.dp)
            pl.semaphore_signal(barrier, inc=1, device_id=peer, device_id_type=MESH)
            return 0

        lax.fori_loop(1, NROWS, one, 0)
        for k in range(1, NDP):
            peer = (self.rows, lax.rem(self.dp + k, NDP))
            pl.semaphore_signal(barrier, inc=1, device_id=peer, device_id_type=MESH)
        pl.semaphore_wait(barrier, NROWS + NDP - 2)


def remote(src, dst, sems, k, device):
    return pltpu.make_async_remote_copy(
        src_ref=src,
        dst_ref=dst,
        send_sem=sems[0].at[k],
        recv_sem=sems[1].at[k],
        device_id=device,
        device_id_type=MESH,
    )


def regroup_quad(c, r):
    quad, m = c.dp // 4 * 4, c.dp % 4
    copies = []
    for k in range(1, 4):
        other = lax.rem(m + k, 4)
        copy = remote(r.wpart.at[other], r.wquad.at[m], r.quad_sems, k, (c.rows, quad + other))
        copy.start()
        copies.append(copy)
    r.wquad[m] = r.wpart[m]
    for copy in copies:
        copy.wait()
    row = lax.broadcasted_iota(jnp.int32, (48, 64), 0)
    col = lax.broadcasted_iota(jnp.int32, (48, 64), 1)
    pick = ((col // 16 * 12 + col % 16 == row) & (col % 16 < 12)).astype(F32).astype(BF16)
    block = jnp.dot(pick, r.wquad[...].reshape(64, 384), preferred_element_type=F32).astype(BF16)
    y = c.pos["y"]
    for j in range(3):
        r.w[y % 2, c.core, c.pos["z"], c.pos["x"], y // 2, j] = block[j * 16 : j * 16 + 16]


def gather_part(c, r, part):
    sems = (r.wsend.at[part], r.wrecv.at[part])
    sent = []
    slot = 0

    def block(core, whole, **at):
        at = {**c.pos, **at}
        z = slice(None) if "z" in whole else at["z"]
        x = slice(None) if "x" in whole else at["x"]
        yl, yh = (slice(None), slice(None)) if "y" in whole else (at["y"] % 2, at["y"] // 2)
        return r.w.at[yl, core, z, x, yh, part]

    order = ORDERS[part]
    for level, axis in enumerate(order):
        whole, n, here = order[:level], SIZE[axis], c.pos[axis]
        last = level == 2

        def at(step):
            return {axis: lax.rem(here + step + 2 * n, n)}

        def push(step, device):
            nonlocal slot
            mine = block(c.core, whole, **at(step))
            copy = remote(mine, mine, sems, slot, device)
            slot += 1
            copy.start()
            sent.append(copy)
            return slot - 1

        def arrived(k, step, core):
            got = block(core, whole, **at(step))
            remote(got, got, sems, k, c.device(core=1 - c.core)).wait_recv()

        siblings = []

        def to_sibling(step):
            if last:
                siblings.append((push(step, c.device(core=1 - c.core)), step))

        for step in range(n // 2):
            if step < n // 2 - 1:
                ahead = push(-step, c.device(**at(1)))
                back = push(step, c.device(**at(-1)))
                if step == 0:
                    to_sibling(0)
                yield
                arrived(ahead, -step - 1, c.core)
                to_sibling(-step - 1)
                arrived(back, step + 1, c.core)
                to_sibling(step + 1)
            else:
                way = 1 - 2 * c.core
                k = push(-way * step, c.device(**at(way)))
                yield
                arrived(k, n // 2, c.core)
                to_sibling(n // 2)
        for k, step in siblings:
            yield
            arrived(k, step, 1 - c.core)
    for copy in sent:
        copy.wait_send()


class Drive:
    def __init__(self, tasks):
        self.tasks = list(tasks)

    def step(self):
        for task in list(self.tasks):
            if next(task, "end") == "end":
                self.tasks.remove(task)

    def finish(self):
        while self.tasks:
            self.step()


def exchange_start(c, src, dst, sems):
    def one(k, _):
        peer = lax.rem(c.rows + k, NROWS)
        remote(
            src.at[pl.ds(peer * 16, 16)], dst.at[pl.ds(c.rows * 16, 16)], sems, k, (peer, c.dp)
        ).start()
        return 0

    lax.fori_loop(1, NROWS, one, 0)
    mine = pl.ds(pl.multiple_of(c.rows * 16, 16), 16)
    dst[mine] = src[mine]


def exchange_wait(c, src, dst, sems):
    def one(k, _):
        peer = lax.rem(c.rows - k + NROWS, NROWS)
        remote(
            src.at[pl.ds(peer * 16, 16)], dst.at[pl.ds(peer * 16, 16)], sems, k, (peer, c.dp)
        ).wait()
        return 0

    lax.fori_loop(1, NROWS, one, 0)


def to_all(c, axis, n, here, src_of, dst, sems, device_of):
    copies = []
    for k in range(1, n):
        other = lax.rem(here + k, n)
        copy = remote(src_of(other), dst.at[here], sems, k, device_of(other))
        copy.start()
        copies.append(copy)
    return copies


def wait_all(copies):
    for copy in copies:
        copy.wait()


def total_of(ref, n):
    total = ref[0]
    for k in range(1, n):
        total = total + ref[k]
    return total


def reduce_sums(c, r):
    x, z = c.pos["x"], c.pos["z"]

    def dp_device(other):
        return (c.rows, other)

    def x_device(other):
        return c.device(x=other)

    def z_device(other):
        return c.device(z=other)

    blocks = r.sums.reshape(NDP, 128, 128)
    copies = to_all(c, "dp", NDP, c.dp, lambda o: blocks.at[o], r.red_a, r.sems_a, dp_device)
    r.red_a[c.dp] = r.sums[pl.ds(pl.multiple_of(c.dp * 128, 128), 128), :]
    wait_all(copies)
    r.sum_a[...] = total_of(r.red_a, NDP).reshape(NX, 32, 128)
    copies = to_all(c, "x", NX, x, lambda o: r.sum_a.at[o], r.red_b, r.sems_b, x_device)
    r.red_b[x] = r.sum_a[x]
    wait_all(copies)
    r.sum_b[...] = total_of(r.red_b, NX)
    copies = to_all(c, "z", NZ, z, lambda o: r.sum_b, r.red_c, r.sems_c, z_device)
    r.red_c[z] = r.sum_b[...]
    wait_all(copies)
    r.sum_c[...] = total_of(r.red_c, NZ)
    copies = to_all(c, "x", NX, x, lambda o: r.sum_c, r.red_d, r.sems_d, x_device)
    r.red_d[x] = r.sum_c[...]
    wait_all(copies)
    copies = to_all(c, "dp", NDP, c.dp, lambda o: r.red_d, r.total, r.sems_e, dp_device)
    r.total[c.dp] = r.red_d[...]
    wait_all(copies)


COMM_SCRATCH = dict(
    w=((2, 2, NZ, NX, 2, 3, 16, 384), BF16),
    wquad=((4, 16, 384), BF16),
    cot_send=((NROWS * 16, 1536), BF16),
    cot_recv=((NROWS * 16, 1536), BF16),
    feat_send=((NROWS * 16, 1536), BF16),
    feat_recv=((NROWS * 16, 1536), BF16),
    sums=((1024, 128), F32),
    red_a=((NDP, 128, 128), F32),
    sum_a=((NX, 32, 128), F32),
    red_b=((NX, 32, 128), F32),
    sum_b=((32, 128), F32),
    red_c=((NZ, 32, 128), F32),
    sum_c=((32, 128), F32),
    red_d=((NX, 32, 128), F32),
)
PAIRS = dict(quad_sems=4, cot_sems=NROWS, feat_sems=NROWS, sems_a=NDP, sems_b=NX, sems_c=NZ, sems_d=NX, sems_e=NDP)
INPUTS = ("xin", "masks", "k2", "b2", "gain", "k3", "b3", "db", "wpart", "cot", "put_cot", "pick_cot", "put_feat", "pick_feat")
OUTPUTS = ("features", "pixel_grad", "total")


def whole_kernel(*refs):
    names = INPUTS + OUTPUTS + tuple(COMPUTE_SCRATCH) + tuple(COMM_SCRATCH)
    r = SimpleNamespace(**dict(zip(names, refs)))
    rest = refs[len(names) :]
    for k, name in enumerate(PAIRS):
        setattr(r, name, (rest[2 * k], rest[2 * k + 1]))
    r.wsend, r.wrecv = rest[2 * len(PAIRS) :]

    c = Comm()
    c.greet()
    regroup_quad(c, r)
    drive = Drive([gather_part(c, r, part) for part in range(3)])
    drive.step()
    for n in range(4):
        at = slice(n * 384, n * 384 + 384)
        r.cot_send[:, at] = jnp.dot(
            r.put_cot[...], r.cot[:, at], preferred_element_type=F32
        ).astype(BF16)
    exchange_start(c, r.cot_send, r.cot_recv, r.cot_sems)
    r.sums[...] = jnp.zeros((1024, 128), F32)
    drive.step()
    spread_taps(r)
    drive.step()
    load_pixels(r)
    for ch in range(6):
        drive.step()
        forward_two(r, ch)
    drive.step()
    norm_two(r)
    drive.finish()
    for n in range(4):
        project(r, n)
    forward_three(r)
    for n in range(4):
        part = jnp.concatenate([r.feat[n * 3 + cb].astype(BF16) for cb in range(3)], axis=1)
        r.feat_send[:, n * 384 : n * 384 + 384] = jnp.dot(
            r.put_feat[...], part, preferred_element_type=F32
        ).astype(BF16)
    exchange_start(c, r.feat_send, r.feat_recv, r.feat_sems)
    exchange_wait(c, r.cot_send, r.cot_recv, r.cot_sems)
    place_cotangent(r)
    backward_three(r)
    for ab in range(4):
        project_back(r, ab)
    kernel_three(r)
    norm_back(r)
    kernel_two(r)
    backward_two(r)
    reduce_sums(c, r)
    exchange_wait(c, r.feat_send, r.feat_recv, r.feat_sems)
    for n in range(4):
        at = slice(n * 384, n * 384 + 384)
        r.features[:, at] = jnp.dot(
            r.pick_feat[...], r.feat_recv[:, at], preferred_element_type=F32
        ).astype(BF16)


def run_kernel(*arrays):
    vmem = pl.BlockSpec(memory_space=pltpu.VMEM)
    scratch = [pltpu.VMEM(*v) for v in COMPUTE_SCRATCH.values()]
    scratch += [pltpu.VMEM(*v) for v in COMM_SCRATCH.values()]
    for n in PAIRS.values():
        scratch += [pltpu.SemaphoreType.DMA((n,))] * 2
    scratch += [pltpu.SemaphoreType.DMA((3, 32))] * 2
    return pl.pallas_call(
        whole_kernel,
        out_shape=(
            jax.ShapeDtypeStruct((256, 1536), BF16),
            jax.ShapeDtypeStruct((16, 32, 768), BF16),
            jax.ShapeDtypeStruct((NDP, NX, 32, 128), F32),
        ),
        in_specs=[vmem] * len(INPUTS),
        out_specs=(vmem,) * 3,
        scratch_shapes=scratch,
        compiler_params=pltpu.CompilerParams(
            collective_id=0, has_side_effects=True, vmem_limit_bytes=60 * 1024 * 1024
        ),
    )(*arrays)


def table_pick(table, index):
    matches = index[..., None] == jnp.arange(table.shape[0], dtype=jnp.int32)
    return jnp.sum(jnp.where(matches, table, 0), axis=-1)


def one_hot(index, size):
    return (index[:, None] == jnp.arange(size, dtype=jnp.int32)[None, :]).astype(BF16)


def pair_rows(hits, starts, ends, first, beyond):
    at = jnp.arange(starts.shape[0], dtype=jnp.int32)
    tile = jnp.sum(jnp.where(hits, at[None, :], 0), axis=1)
    present = jnp.any(hits, axis=1)
    low = jnp.maximum(table_pick(starts, tile), first)
    high = jnp.minimum(table_pick(ends, tile), beyond)
    return tile, low, jnp.where(present, high, low)


def tables(heights, widths, owners, here):
    order = jnp.arange(heights.shape[0], dtype=jnp.int32)
    upto = order[None, :] <= order[:, None]
    ends = jnp.sum(jnp.where(upto, heights[None, :], 0), axis=1)
    starts = ends - heights
    earlier = (owners[:, None] == owners[None, :]) & (order[None, :] < order[:, None])
    own_start = jnp.sum(jnp.where(earlier, heights[None, :], 0), axis=1)
    total = NROWS * 32
    rows = here * 32 - OWN + jnp.arange(WIN, dtype=jnp.int32)
    inside = jnp.sum((starts[None, :] <= rows[:, None]).astype(jnp.int32), axis=1) - 1
    tile = jnp.where((rows >= 0) & (rows < total), inside, -1)
    width = table_pick(widths, tile) // 2
    wide = jnp.pad(tile, (3, 3), constant_values=-1)
    same = jnp.stack([wide[k : k + WIN] == tile for k in range(7)])
    columns = width[None, :] > jnp.arange(4, dtype=jnp.int32)[:, None]
    masks = jnp.concatenate([same, columns]).astype(F32)
    masks = jnp.broadcast_to(masks[:, :, None], (11, WIN, 128))
    peers = jnp.arange(NROWS, dtype=jnp.int32)
    k4 = jnp.arange(4, dtype=jnp.int32)
    low = peers * 32 - 8
    hits = (
        (owners[None, :] == here) & (starts[None, :] < low[:, None] + 48) & (ends[None, :] > low[:, None])
    )
    t, lo, hi = pair_rows(hits, starts, ends, low, low + 48)
    row = lo[:, None] + k4[None, :]
    own = table_pick(own_start, t)[:, None] + row - table_pick(starts, t)[:, None]
    own = jnp.where(row < hi[:, None], own, -1024)
    put_cot = one_hot((own[:, :, None] * 4 + k4[None, None, :]).reshape(-1), 256)
    first = jnp.maximum(table_pick(starts, tile), here * 32 - 8)
    source = table_pick(owners, tile) * 16 + (rows - first) * 4
    source = jnp.where((rows >= here * 32 - 8) & (rows < here * 32 + 40), source, -1024)
    source = source[None, :] + k4[:, None]
    pick_cot = one_hot(jnp.where(columns, source, -1024).reshape(-1), NROWS * 16)
    low = here * 32
    hits = (owners[None, :] == peers[:, None]) & (starts[None, :] < low + 32) & (ends[None, :] > low)
    t, lo, hi = pair_rows(hits, starts, ends, low, low + 32)
    row = lo[:, None] + k4[None, :]
    row = jnp.where(row < hi[:, None], row - low, -1024)
    put_feat = one_hot((row[:, :, None] + 32 * k4[None, None, :]).reshape(-1), 128)
    slot = jnp.arange(64, dtype=jnp.int32)
    hits = (
        (owners[None, :] == here)
        & (own_start[None, :] <= slot[:, None])
        & (slot[:, None] < (own_start + heights)[None, :])
    )
    t = jnp.sum(jnp.where(hits, order[None, :], 0), axis=1)
    begin = table_pick(starts, t)
    row = begin + slot - table_pick(own_start, t)
    device = row // 32
    source = device * 16 + (row - jnp.maximum(begin, device * 32)) * 4
    source = jnp.where(jnp.any(hits, axis=1), source, -1024)
    pick_feat = one_hot((source[:, None] + k4[None, :]).reshape(-1), NROWS * 16)
    return masks, put_cot, pick_cot, put_feat, pick_feat


def window_pixels(before, own, after):
    ext = jnp.concatenate([before, own, after], axis=0)
    ext = ext.reshape(48, 2, 8, 768).transpose(1, 2, 0, 3).reshape(16, 48, 768)
    return jnp.pad(ext, ((0, 0), (4, 4), (0, 0)))


def body(
    pixels,
    kernel_two,
    bias_two,
    gain_two,
    down_weight,
    down_bias,
    kernel_three,
    bias_three,
    cotangent,
    tile_height,
    tile_width,
    tile_owner,
):
    own = pixels[0]
    here = lax.axis_index("rows")
    ends = NROWS - 1
    before = lax.ppermute(own[48:], "rows", [(i, i + 1) for i in range(ends)])
    after = lax.ppermute(own[:16], "rows", [(i + 1, i) for i in range(ends)])
    masks, put_cot, pick_cot, put_feat, pick_feat = tables(
        tile_height[0], tile_width[0], tile_owner[0], here
    )
    xin = window_pixels(before, own, after)
    wpart = jnp.pad(down_weight.reshape(12, 4, 384).transpose(1, 0, 2), ((0, 0), (0, 4), (0, 0)))
    features, pixel_grad, total = run_kernel(
        xin,
        masks,
        kernel_two,
        bias_two[None],
        gain_two[None],
        kernel_three,
        bias_three[None],
        down_bias[None],
        wpart,
        cotangent[0].reshape(256, 1536),
        put_cot,
        pick_cot,
        put_feat,
        pick_feat,
    )
    pixel_grad = pixel_grad.reshape(2, 8, 32, 768).transpose(2, 0, 1, 3).reshape(1, 64, 8, 768)
    factor = 1.0 / math.sqrt(NROWS * NDP * 64 * 8)
    sums = total.reshape(1024, 128)[:1008].reshape(18, 56, 128) * factor
    two = sums[:6].transpose(1, 0, 2).reshape(56, 768)
    three = sums[6:].transpose(1, 0, 2).reshape(56, 1536)
    return (
        features.reshape(1, 64, 4, 1536),
        pixel_grad,
        two[:49],
        two[49],
        two[50],
        three[:49],
        three[49],
    )


def solution(mesh):
    in_specs = (
        P("dp", "rows", None, None),
        P(),
        P(),
        P(),
        P(("rows", "dp"), None),
        P(),
        P(),
        P(),
        P("dp", "rows", None, None),
        P("dp", None),
        P("dp", None),
        P("dp", None),
    )
    out_specs = (P("dp", "rows", None, None), P("dp", "rows", None, None), P(), P(), P(), P(), P())
    return jax.shard_map(body, mesh=mesh, in_specs=in_specs, out_specs=out_specs, check_vma=False)
```

```python
import functools
import math
from types import SimpleNamespace

import jax
import jax.numpy as jnp
from jax import lax
from jax.experimental import pallas as pl
from jax.experimental.pallas import tpu as pltpu
from jax.sharding import PartitionSpec as P

MESH = pl.DeviceIdType.MESH
F32 = jnp.float32
BF16 = jnp.bfloat16
epsilon = 1e-06

NZ, NX, NY = 8, 4, 4
NROWS = NZ * NX
NDP = 2 * NY
SIZE = {"x": NX, "y": NY, "z": NZ}
PARTS = ((0, 0, 384, "zxy"), (1, 0, 384, "zyx"), (2, 0, 384, "zxy"))
WIN = 56
OWN = 12
BASE = 8
ROWS_TWO = 40
ROWS_THREE = 96


def iota_of(shape, dim):
    return lax.broadcasted_iota(jnp.int32, shape, dim)


def as_row(column):
    n = column.shape[0]
    eye = iota_of((n, n), 0) == iota_of((n, n), 1)
    return jnp.sum(jnp.where(eye, column, 0.0), axis=0, keepdims=True)


def as_column(row):
    n = row.shape[1]
    eye = iota_of((n, n), 0) == iota_of((n, n), 1)
    return jnp.sum(jnp.where(eye, row, 0.0), axis=1, keepdims=True)


def make_tables(c, r):
    n = r.heights.shape[1]
    heights, widths, owners = (
        ref[...].astype(F32) for ref in (r.heights, r.widths, r.owners)
    )
    before, after = iota_of((n, n), 0), iota_of((n, n), 1)
    lengths = jnp.broadcast_to(heights, (16, n)).astype(BF16)
    ends = jnp.dot(lengths, one_hot(before <= after), preferred_element_type=F32)[0:1]
    starts = ends - heights
    earlier = one_hot((as_column(owners) == owners) & (before < after))
    own_start = jnp.dot(lengths, earlier, preferred_element_type=F32)[0:1]

    def add(hits, table):
        return jnp.sum(jnp.where(hits, table, 0.0), axis=1, keepdims=True)

    row = (c.rows * 32 - OWN + iota_of((WIN, n), 0)).astype(F32)
    hits = (starts <= row) & (row < ends)
    tile = add(hits, (iota_of((WIN, n), 1) + 1).astype(F32))
    width = jnp.broadcast_to(add(hits, widths), (WIN, 128))
    r.tile[...] = jnp.zeros((WIN + 16, 128), F32)
    r.tile[8 : 8 + WIN, :] = jnp.broadcast_to(tile, (WIN, 128))
    here = r.tile[8 : 8 + WIN, :]
    for k in range(7):
        there = r.tile[5 + k : 5 + k + WIN, :]
        r.masks[k] = jnp.where(there == here, 1.0, 0.0)
    for q in range(4):
        r.masks[7 + q] = jnp.where(width > 2.0 * q, 1.0, 0.0)
    z, x = c.pos["z"], c.pos["x"]
    line = iota_of((256, n), 0)
    strip = z * 128 + x + 4 * (line // 8)
    hits = (starts <= strip.astype(F32)) & (strip.astype(F32) < ends)
    line = iota_of((256, 1), 0)
    strip = z * 128 + x + 4 * (line // 8)
    at = (add(hits, owners).astype(jnp.int32) * 2 + strip // 64 % 2) * 8 + line % 8
    r.strip_col[...] = at
    r.strip_row[...] = as_row(at.astype(F32)).astype(jnp.int32)
    own = (iota_of((256, n), 0) // 4).astype(F32)
    hits = (owners == c.rows.astype(F32)) & (own_start <= own) & (own < own_start + heights)
    row = add(hits, starts - own_start).astype(jnp.int32) + line // 4
    at = ((row // 128 * NX + row % 4) * 2 + row // 64 % 2) * 8 + 2 * (line % 4)
    at = jnp.where(add(hits, 1.0) > 0.0, at, -1024)
    r.own_col[...] = at
    r.own_row[...] = as_row(at.astype(F32)).astype(jnp.int32)


def load_parameters(r):
    r.par2[0:49, :] = r.k2[...]
    r.par2[49:50, :] = r.b2[...].reshape(1, 768)
    r.par2[50:51, :] = r.gain[...].reshape(1, 768)
    r.par3[0:49, :] = r.k3[...]
    r.par3[49:50, :] = r.b3[...].reshape(1, 1536)
    r.par3[50:51, :] = r.db[...].reshape(1, 1536)
    r.wpart[...] = jnp.zeros((4, 16, 384), BF16)
    for k in range(4):
        r.wpart[k, 0:12, :] = r.weight[:, k * 384 : k * 384 + 384]


def spread_taps(r):
    def one(t, _):
        row = r.par2[pl.ds(t, 1), :]
        for ch in range(6):
            r.kb2[ch, t] = jnp.broadcast_to(row[:, ch * 128 : ch * 128 + 128], (8, 128))
        row = r.par3[pl.ds(t, 1), :]
        for ch in range(12):
            r.kb3[ch, t] = jnp.broadcast_to(row[:, ch * 128 : ch * 128 + 128], (8, 128))
        return 0

    lax.fori_loop(0, 50, one, 0)


def iotas(rows, cols):
    return (
        lax.broadcasted_iota(jnp.int32, (rows, cols), 0),
        lax.broadcasted_iota(jnp.int32, (rows, cols), 1),
    )


def one_hot(hit):
    return jnp.where(hit, 1.0, 0.0).astype(BF16)


def turn(back):
    row, col = iotas(128, 128)
    if back:
        row, col = col, row
    ac = row // 8
    return one_hot(col == (2 * (row % 8) + ac // 8) * 8 + ac % 8)


def load_pixels(r, lines, group):
    block = jnp.dot(turn(False), lines, preferred_element_type=F32)
    s0 = 4 + 8 * group
    for ac in range(16):
        inside = r.masks[7 + (ac % 8) // 2, s0 : s0 + 8, :]
        for ch in range(6):
            part = block[ac * 8 : ac * 8 + 8, ch * 128 : ch * 128 + 128]
            r.x[ch, ac, s0 : s0 + 8, :] = part * inside


def conv2(r, src, ch, a, s0, flip, accs):
    for i in range(7):
        t = a + i - 3
        par, shift = t % 2, t // 2
        cols = [src[ch, par * 8 + c, pl.ds(s0 + shift, 8), :] for c in range(8)]
        if shift != 0:
            same = r.masks[shift + 3, pl.ds(s0, 8), :]
            cols = [v * same for v in cols]
        for j in range(7):
            tap = 7 * i + j
            k = r.kb2[ch, 48 - tap if flip else tap]
            for c in range(8):
                if 0 <= c + j - 3 < 8:
                    term = cols[c + j - 3] * k
                    accs[c] = term if accs[c] is None else accs[c] + term
    return accs


def conv3(r, src, ch, s0, flip, accs):
    for i in range(7):
        cols = [src[ch, q, pl.ds(s0 + i - 3, 8), :] for q in range(4)]
        if i != 3:
            same = r.masks[i, pl.ds(s0, 8), :]
            cols = [v * same for v in cols]
        for j in range(7):
            tap = 7 * i + j
            k = r.kb3[ch, 48 - tap if flip else tap]
            for q in range(4):
                if 0 <= q + j - 3 < 4:
                    term = cols[q + j - 3] * k
                    accs[q] = term if accs[q] is None else accs[q] + term
    return accs


def forward_two(r, ch):
    def block(b, _):
        s0 = BASE + 8 * b
        for a in range(2):
            accs = conv2(r, r.x, ch, a, s0, False, [r.kb2[ch, 49]] * 8)
            for c in range(8):
                r.act[ch, a * 8 + c, pl.ds(8 * b, 8), :] = accs[c]
        return 0

    lax.fori_loop(0, 5, block, 0)


def channel_mean(parts):
    total = parts[0]
    for v in parts[1:]:
        total = total + v
    return jnp.sum(total, axis=1, keepdims=True) * (1.0 / 768)


def norm_two(r, low, high):
    def one(ac, _):
        a, col = ac // 8, ac % 8
        q, b2 = col // 2, col % 2
        for b in range(5):
            inside = r.masks[7 + q, pl.ds(BASE + 8 * b, 8), :]
            act = [r.act[ch, ac, 8 * b : 8 * b + 8, :] * inside for ch in range(6)]
            mean = channel_mean(act)
            act = [v - mean for v in act]
            inverse = lax.rsqrt(channel_mean([v * v for v in act]) + epsilon)
            r.inv[ac, 8 * b : 8 * b + 8, :] = jnp.broadcast_to(inverse, (8, 128))
            for ch in range(6):
                nhat = act[ch] * inverse
                r.act[ch, ac, 8 * b : 8 * b + 8, :] = nhat
                gain = r.par2[50:51, ch * 128 : ch * 128 + 128]
                r.lhs[a * 2 + b2, pl.ds(q * 40 + 8 * b, 8), ch * 128 : ch * 128 + 128] = nhat * gain
        return 0

    lax.fori_loop(low, high, one, 0)


def weight_panel(r, n, ab):
    return r.w[n // 2, n % 2, pl.ds(2 * ab, 2)].reshape(768, 384)


def project(r, n):
    total = jnp.zeros((160, 384), F32)
    for ab in range(4):
        total = total + jnp.dot(
            r.lhs[ab].astype(BF16), weight_panel(r, n, ab), preferred_element_type=F32
        )
    for cb in range(3):
        ch = n * 3 + cb
        bias = r.par3[50:51, ch * 128 : ch * 128 + 128]
        for q in range(4):
            part = total[q * 40 : q * 40 + 40, cb * 128 : cb * 128 + 128] + bias
            part = part * r.masks[7 + q, BASE : BASE + 40, :]
            r.down[ch, q, BASE : BASE + 40, :] = part.astype(BF16).astype(F32)


def forward_three(r):
    def one(ch, _):
        for b in range(4):
            s0 = OWN + 8 * b
            accs = conv3(r, r.down, ch, s0, False, [r.kb3[ch, 49]] * 4)
            for q in range(4):
                inside = r.masks[7 + q, s0 : s0 + 8, :]
                out = r.down[ch, q, s0 : s0 + 8, :] + accs[q] * inside
                r.feat[ch, q * 32 + 8 * b : q * 32 + 8 * b + 8, :] = out
        return 0

    lax.fori_loop(0, 12, one, 0)


def pack_features(r):
    row, col = iotas(256, 128)
    at = (row // 2 % 4) * 32 + (row // 8 % 8) * 4 + row // 64
    total = jnp.zeros((256, 768), F32)
    for half in range(2):
        pick = one_hot((col == at) & (row % 2 == half))
        part = jnp.concatenate(
            [r.feat[half * 6 + k].astype(BF16) for k in range(6)], axis=1
        )
        total = total + jnp.dot(pick, part, preferred_element_type=F32)
    r.feat_out[...] = total.astype(BF16).reshape(4, 64, 768)


def place_cotangent(r):
    row, col = iotas(4 * WIN, 384)
    own = col - 64
    edge = (col % 16 // 8) * 4 + jnp.where(col < 64, col // 16 - 8, (col - 320) // 16 + 32)
    mid = (own % 64 // 8) * 4 + own // 64
    p = jnp.where((col >= 64) & (col < 320), mid, edge)
    line = (col % 8 // 2) * WIN + p + OWN
    lines = jnp.concatenate(
        [r.cot_left[...].reshape(64, 768), r.cot_own[...].reshape(256, 768), r.cot_right[...].reshape(64, 768)],
        axis=0,
    )
    for half in range(2):
        pick = one_hot((row == line) & (col % 2 == half))
        part = jnp.dot(pick, lines, preferred_element_type=F32)
        for k in range(6):
            for q in range(4):
                block = part[q * WIN : q * WIN + WIN, k * 128 : k * 128 + 128]
                r.gout[half * 6 + k, q] = block * r.masks[7 + q]


def backward_three(r):
    def one(ch, _):
        for b in range(5):
            s0 = BASE + 8 * b
            accs = conv3(r, r.gout, ch, s0, True, [None] * 4)
            for q in range(4):
                inside = r.masks[7 + q, s0 : s0 + 8, :]
                out = (r.gout[ch, q, s0 : s0 + 8, :] + accs[q]) * inside
                r.gdown[ch, q * 40 + 8 * b : q * 40 + 8 * b + 8, :] = out
        return 0

    lax.fori_loop(0, 12, one, 0)


def row_sum(v):
    return jnp.sum(v, axis=0, keepdims=True)


def kernel_three(r, low, high):
    def one(ch, _):
        bias = None
        for i in range(7):
            accs = [None] * 7
            for b in range(4):
                s0 = OWN + 8 * b
                grads = [r.gout[ch, q, s0 : s0 + 8, :] for q in range(4)]
                if i == 0:
                    for v in grads:
                        bias = v if bias is None else bias + v
                if i != 3:
                    same = r.masks[i, s0 : s0 + 8, :]
                    grads = [v * same for v in grads]
                field = [r.down[ch, q, s0 + i - 3 : s0 + i + 5, :] for q in range(4)]
                for j in range(7):
                    for q in range(4):
                        if 0 <= q + j - 3 < 4:
                            term = grads[q] * field[q + j - 3]
                            accs[j] = term if accs[j] is None else accs[j] + term
            for j in range(7):
                r.sums3[pl.ds(ch * 50 + 7 * i + j, 1), :] = row_sum(accs[j])
        r.sums3[pl.ds(ch * 50 + 49, 1), :] = row_sum(bias)
        return 0

    lax.fori_loop(low, high, one, 0)


def project_back(r, ab):
    total = jnp.zeros((160, 768), F32)
    for n in range(4):
        part = jnp.concatenate([r.gdown[n * 3 + cb].astype(BF16) for cb in range(3)], axis=1)
        total = total + lax.dot_general(
            part, weight_panel(r, n, ab), (((1,), (1,)), ((), ())), preferred_element_type=F32
        )
    r.lhs[ab] = total.astype(BF16).astype(F32)


def norm_back(r):
    zeros = jnp.zeros((8, 128), F32)

    def one(ac, carry):
        carry = list(carry)
        a, col = ac // 8, ac % 8
        q, b2 = col // 2, col % 2
        row = lax.broadcasted_iota(jnp.int32, (8, 128), 0)
        for b in range(5):
            inside = r.masks[7 + q, pl.ds(BASE + 8 * b, 8), :]
            inverse = r.inv[ac, 8 * b : 8 * b + 8, :] * inside
            nhat = [r.act[ch, ac, 8 * b : 8 * b + 8, :] for ch in range(6)]
            gn = [
                r.lhs[a * 2 + b2, pl.ds(q * 40 + 8 * b, 8), ch * 128 : ch * 128 + 128]
                for ch in range(6)
            ]
            scaled = [gn[ch] * r.par2[50:51, ch * 128 : ch * 128 + 128] for ch in range(6)]
            mean = channel_mean(scaled)
            mixed = channel_mean([s * v for s, v in zip(scaled, nhat)])
            for ch in range(6):
                grad = inverse * (scaled[ch] - mean - nhat[ch] * mixed)
                grad = grad.astype(BF16).astype(F32)
                r.gact[ch, ac, BASE + 8 * b : BASE + 8 * b + 8, :] = grad
                gain_term = gn[ch] * nhat[ch]
                if b in (0, 4):
                    keep = row >= 4 if b == 0 else row < 4
                    gain_term = jnp.where(keep, gain_term, 0.0)
                    grad = jnp.where(keep, grad, 0.0)
                carry[ch] = carry[ch] + grad
                carry[6 + ch] = carry[6 + ch] + gain_term
        return tuple(carry)

    sums = lax.fori_loop(0, 16, one, (zeros,) * 12)
    for ch in range(6):
        r.sums2[ch * 51 + 49 : ch * 51 + 50, :] = row_sum(sums[ch])
        r.sums2[ch * 51 + 50 : ch * 51 + 51, :] = row_sum(sums[6 + ch])


def kernel_two(r, low, high):
    def one(ch, _):
        for i in range(7):
            accs = [None] * 7
            for a in range(2):
                t = a + i - 3
                par, shift = t % 2, t // 2
                for b in range(4):
                    s0 = OWN + 8 * b
                    grads = [r.gact[ch, a * 8 + c, s0 : s0 + 8, :] for c in range(8)]
                    if shift != 0:
                        same = r.masks[shift + 3, s0 : s0 + 8, :]
                        grads = [v * same for v in grads]
                    field = [
                        r.x[ch, par * 8 + c, s0 + shift : s0 + shift + 8, :] for c in range(8)
                    ]
                    for j in range(7):
                        for c in range(8):
                            if 0 <= c + j - 3 < 8:
                                term = grads[c] * field[c + j - 3]
                                accs[j] = term if accs[j] is None else accs[j] + term
            for j in range(7):
                r.sums2[pl.ds(ch * 51 + 7 * i + j, 1), :] = row_sum(accs[j])
        return 0

    lax.fori_loop(low, high, one, 0)


def backward_two(r, low, high):
    def one(ch, _):
        for b in range(4):
            s0 = OWN + 8 * b
            for a in range(2):
                accs = conv2(r, r.gact, ch, a, s0, True, [None] * 8)
                for c in range(8):
                    inside = r.masks[7 + c // 2, s0 : s0 + 8, :]
                    at = (a * 8 + c) * 8
                    r.pgrad[b, ch, at : at + 8, :] = accs[c] * inside
        return 0

    lax.fori_loop(low, high, one, 0)


def store_pixel_grad(r):
    for b in range(4):
        lines = jnp.concatenate([r.pgrad[b, ch].astype(BF16) for ch in range(6)], axis=1)
        out = jnp.dot(turn(True), lines, preferred_element_type=F32)
        r.pixel_grad[b * 128 : b * 128 + 128, :] = out.astype(BF16)


COMPUTE_SCRATCH = dict(
    masks=((11, WIN, 128), F32),
    tile=((WIN + 16, 128), F32),
    par2=((56, 768), F32),
    par3=((56, 1536), F32),
    own_row=((1, 256), jnp.int32),
    own_col=((256, 1), jnp.int32),
    strip_row=((1, 256), jnp.int32),
    strip_col=((256, 1), jnp.int32),
    kb2=((6, 50, 8, 128), F32),
    kb3=((12, 50, 8, 128), F32),
    x=((6, 16, WIN, 128), F32),
    act=((6, 16, 40, 128), F32),
    inv=((16, 40, 128), F32),
    lhs=((4, 160, 768), F32),
    down=((12, 4, WIN, 128), F32),
    feat=((12, 128, 128), F32),
    gout=((12, 4, WIN, 128), F32),
    gdown=((12, 160, 128), F32),
    gact=((6, 16, WIN, 128), F32),
    pgrad=((4, 6, 128, 128), F32),
)


class Comm:
    def __init__(self):
        rows, dp = lax.axis_index("rows"), lax.axis_index("dp")
        self.rows, self.dp = rows, dp
        self.pos = {"z": rows // NX, "x": rows % NX, "y": dp // 2}
        self.core = dp % 2

    def device(self, **moved):
        at = {**self.pos, "core": self.core, **moved}
        return (at["z"] * NX + at["x"], at["y"] * 2 + at["core"])

    def greet(self):
        barrier = pltpu.get_barrier_semaphore()

        def one(k, _):
            peer = (lax.rem(self.rows + k, NROWS), self.dp)
            pl.semaphore_signal(barrier, inc=1, device_id=peer, device_id_type=MESH)
            return 0

        lax.fori_loop(1, NROWS, one, 0)
        for k in range(1, NDP):
            peer = (self.rows, lax.rem(self.dp + k, NDP))
            pl.semaphore_signal(barrier, inc=1, device_id=peer, device_id_type=MESH)

    def met(self):
        pl.semaphore_wait(pltpu.get_barrier_semaphore(), NROWS + NDP - 2)


def remote(src, dst, sems, k, device):
    return pltpu.make_async_remote_copy(
        src_ref=src,
        dst_ref=dst,
        send_sem=sems[0].at[k],
        recv_sem=sems[1].at[k],
        device_id=device,
        device_id_type=MESH,
    )


def wait_all(copies):
    for copy in copies:
        copy.wait()


def regroup_quad(c, r):
    quad, m = c.dp // 4 * 4, c.dp % 4
    copies = []
    for k in range(1, 4):
        other = lax.rem(m + k, 4)
        copy = remote(r.wpart.at[other], r.wquad.at[m], r.quad_sems, k, (c.rows, quad + other))
        copy.start()
        copies.append(copy)
    r.wquad[m] = r.wpart[m]
    yield
    wait_all(copies)
    row, col = iotas(48, 64)
    pick = one_hot((col // 16 * 12 + col % 16 == row) & (col % 16 < 12))
    block = jnp.dot(pick, r.wquad[...].reshape(64, 384), preferred_element_type=F32).astype(BF16)
    y = c.pos["y"]
    for j in range(3):
        r.w[y % 2, c.core, c.pos["z"], c.pos["x"], y // 2, j] = block[j * 16 : j * 16 + 16]


def gather_part(c, r, part):
    sub, lane, lanes, order = PARTS[part]
    sems = (r.wsend.at[part], r.wrecv.at[part])
    sent = []

    def block(core, whole, cut=slice(None), **at):
        at = {**c.pos, **at}
        z = cut if "z" in whole else at["z"]
        x = at["x"] if "x" not in whole else slice(None) if "z" in whole else cut
        yl, yh = (slice(None), slice(None)) if "y" in whole else (at["y"] % 2, at["y"] // 2)
        return r.w.at[yl, core, z, x, yh, sub, :, pl.ds(lane, lanes)]

    def push(mine, device):
        copy = remote(mine, mine, sems, len(sent), device)
        copy.start()
        sent.append(copy)
        return len(sent) - 1

    def arrived(k, got):
        remote(got, got, sems, k, c.device(core=1 - c.core)).wait_recv()

    for level in range(2):
        axis, whole = order[level], order[:level]
        n, here = SIZE[axis], c.pos[axis]
        slots = [
            push(block(c.core, whole), c.device(**{axis: lax.rem(here + k, n)})) for k in range(1, n)
        ]
        yield
        for k, slot in enumerate(slots):
            arrived(slot, block(c.core, whole, **{axis: lax.rem(here + n - 1 - k, n)}))
    axis, whole = order[2], order[:2]
    here, n = c.pos[axis], SIZE[axis]
    way = 1 - 2 * c.core
    sibling = c.device(core=1 - c.core)
    half = (NZ if "z" in whole else NX) // 2
    cuts = [pl.ds(0, half), pl.ds(half, half)]
    family = []

    def at(step):
        return {axis: lax.rem(here + step + 2 * n, n)}

    def mine(step, cut):
        return block(c.core, whole, cut, **at(step))

    def send(step, ahead, cut):
        return push(mine(step, cut), c.device(**at(ahead)))

    def share(step, cut):
        family.append((push(mine(step, cut), sibling), -step, cut))

    moving = {}
    for k, cut in enumerate(cuts):
        moving[k] = (send(0, way, cut), send(0, -way, cut))
    for cut in cuts:
        share(0, cut)
    for step in range(1, n // 2 + 1):
        for k, cut in enumerate(cuts):
            yield
            if step == n // 2:
                arrived(moving[k], mine(step, cut))
                family.append((push(mine(step, cut), sibling), step, cut))
                continue
            ahead, back = moving[k]
            arrived(ahead, mine(-way * step, cut))
            if step == n // 2 - 1:
                moving[k] = send(-way * step, way, cut)
            else:
                again = send(-way * step, way, cut)
            share(-way * step, cut)
            arrived(back, mine(way * step, cut))
            if step < n // 2 - 1:
                moving[k] = (again, send(way * step, -way, cut))
            share(way * step, cut)
    yield
    for slot, step, cut in family:
        arrived(slot, block(1 - c.core, whole, cut, **at(step)))
    for copy in sent:
        copy.wait_send()


def exchange_start(c, src, dst, sems):
    def one(k, _):
        peer = lax.rem(c.rows + k, NROWS)
        remote(
            src.at[pl.ds(peer * 16, 16)], dst.at[pl.ds(c.rows * 16, 16)], sems, k, (peer, c.dp)
        ).start()
        return 0

    lax.fori_loop(1, NROWS, one, 0)
    mine = pl.ds(pl.multiple_of(c.rows * 16, 16), 16)
    dst[mine] = src[mine]


def exchange_wait(c, src, dst, sems):
    def one(k, _):
        peer = lax.rem(c.rows - k + NROWS, NROWS)
        remote(
            src.at[pl.ds(peer * 16, 16)], dst.at[pl.ds(peer * 16, 16)], sems, k, (peer, c.dp)
        ).wait()
        return 0

    lax.fori_loop(1, NROWS, one, 0)


def to_all(n, here, src_of, dst, sems, device_of):
    copies = []
    for k in range(1, n):
        other = lax.rem(here + k, n)
        copy = remote(src_of(other), dst.at[here], sems, k, device_of(other))
        copy.start()
        copies.append(copy)
    return copies


def neighbours(c):
    return (
        (lax.rem(c.rows + NROWS - 1, NROWS), c.dp),
        (lax.rem(c.rows + 1, NROWS), c.dp),
    )


def pixel_halo(c, r):
    left, right = neighbours(c)
    copies = [
        remote(r.pix.at[pl.ds(0, 80)], r.pix_right.at[pl.ds(0, 80)], r.pix_sems, 0, left),
        remote(r.pix.at[pl.ds(432, 80)], r.pix_left.at[pl.ds(48, 80)], r.pix_sems, 1, right),
    ]
    for copy in copies:
        copy.start()
    r.pix_left[0:48] = jnp.zeros((48, 768), BF16)
    r.pix_right[80:128] = jnp.zeros((48, 768), BF16)
    return copies


def pack_cotangent(r):
    row, _ = iotas(512, 256)
    total = jnp.zeros((512, 768), F32)
    for half in range(2):
        pick = one_hot(row == r.own_row[...] + half)
        total = total + jnp.dot(
            pick, r.cot[:, half * 768 : half * 768 + 768], preferred_element_type=F32
        )
    r.cot_send[...] = total.astype(BF16)


def bring_cotangent(c, r):
    x = c.pos["x"]
    exchange_start(c, r.cot_send, r.cot_recv, r.cot_sems)
    yield
    exchange_wait(c, r.cot_send, r.cot_recv, r.cot_sems)
    _, col = iotas(256, 512)
    pick = one_hot(col == r.strip_col[...])
    lines = jnp.dot(pick, r.cot_recv[...], preferred_element_type=F32).astype(BF16)
    r.cot_mid[...] = lines.reshape(4, 64, 768)
    copies = to_all(
        NX, x, lambda o: r.cot_mid.at[o], r.cot_own, r.line_sems, lambda o: c.device(x=o)
    )
    r.cot_own[x] = r.cot_mid[x]
    yield
    wait_all(copies)
    left, right = neighbours(c)
    copies = [
        remote(r.cot_own.at[:, pl.ds(0, 16)], r.cot_right, r.edge_sems, 0, left),
        remote(r.cot_own.at[:, pl.ds(48, 16)], r.cot_left, r.edge_sems, 1, right),
    ]
    for copy in copies:
        copy.start()
    yield
    wait_all(copies)


def take_features(c, r):
    x = c.pos["x"]
    copies = to_all(
        NX, x, lambda o: r.feat_out.at[o], r.feat_mid, r.out_sems, lambda o: c.device(x=o)
    )
    r.feat_mid[x] = r.feat_out[x]
    yield
    wait_all(copies)
    row, _ = iotas(512, 256)
    pick = one_hot(row == r.strip_row[...])
    r.feat_send[...] = jnp.dot(
        pick, r.feat_mid[...].reshape(256, 768), preferred_element_type=F32
    ).astype(BF16)
    exchange_start(c, r.feat_send, r.feat_recv, r.feat_sems)
    yield
    exchange_wait(c, r.feat_send, r.feat_recv, r.feat_sems)
    _, col = iotas(256, 512)
    for half in range(2):
        pick = one_hot(col == r.own_col[...] + half)
        lines = jnp.dot(pick, r.feat_recv[...], preferred_element_type=F32)
        r.features[:, :, half * 768 : half * 768 + 768] = lines.reshape(64, 4, 768).astype(BF16)


def total_of(ref, n):
    total = ref[0]
    for k in range(1, n):
        total = total + ref[k]
    return total


def reduce_sums(c, r, which):
    sums, red_a, red_b, red_c, out, sems = (
        getattr(r, name + which) for name in ("sums", "red_a", "red_b", "red_c", "total", "sems")
    )
    x, z = c.pos["x"], c.pos["z"]
    size = sums.shape[0] // NDP
    split = red_b.shape[1] < size

    def family(k):
        return (sems[0].at[k], sems[1].at[k])

    def dp_device(other):
        return (c.rows, other)

    def x_device(other):
        return c.device(x=other)

    blocks = sums.reshape(NDP, size, 128)
    copies = to_all(NDP, c.dp, lambda o: blocks.at[o], red_a, family(0), dp_device)
    red_a[c.dp] = sums[pl.ds(pl.multiple_of(c.dp * size, 8), size), :]
    yield
    wait_all(copies)
    if split:
        r.part3[...] = total_of(red_a, NDP).reshape(NX, size // NX, 128)
        copies = to_all(NX, x, lambda o: r.part3.at[o], red_b, family(1), x_device)
        red_b[x] = r.part3[x]
    else:
        red_b[x] = total_of(red_a, NDP)
        copies = to_all(NX, x, lambda o: red_b.at[x], red_b, family(1), x_device)
    yield
    wait_all(copies)
    red_c[z] = total_of(red_b, NX)
    copies = to_all(NZ, z, lambda o: red_c.at[z], red_c, family(2), lambda o: c.device(z=o))
    yield
    wait_all(copies)
    if split:
        r.whole3[x] = total_of(red_c, NZ)
        copies = to_all(NX, x, lambda o: r.whole3.at[x], r.whole3, family(4), x_device)
        yield
        wait_all(copies)
        out[c.dp] = r.whole3[...].reshape(size, 128)
    else:
        out[c.dp] = total_of(red_c, NZ)
    copies = to_all(NDP, c.dp, lambda o: out.at[c.dp], out, family(3), dp_device)
    yield
    wait_all(copies)


class Drive:
    def __init__(self, *tasks):
        self.tasks = list(tasks)

    def step(self):
        for task in list(self.tasks):
            if next(task, "end") == "end":
                self.tasks.remove(task)

    def finish(self):
        while self.tasks:
            self.step()


COMM_SCRATCH = dict(
    w=((2, 2, NZ, NX, 2, 3, 16, 384), BF16),
    wpart=((4, 16, 384), BF16),
    wquad=((4, 16, 384), BF16),
    pix_left=((128, 768), BF16),
    pix_right=((128, 768), BF16),
    cot_send=((NROWS * 16, 768), BF16),
    cot_recv=((NROWS * 16, 768), BF16),
    cot_mid=((4, 64, 768), BF16),
    cot_own=((4, 64, 768), BF16),
    cot_left=((4, 16, 768), BF16),
    cot_right=((4, 16, 768), BF16),
    feat_out=((4, 64, 768), BF16),
    feat_mid=((4, 64, 768), BF16),
    feat_send=((NROWS * 16, 768), BF16),
    feat_recv=((NROWS * 16, 768), BF16),
    sums2=((NDP * ROWS_TWO, 128), F32),
    red_a2=((NDP, ROWS_TWO, 128), F32),
    red_b2=((NX, ROWS_TWO, 128), F32),
    red_c2=((NZ, ROWS_TWO, 128), F32),
    sums3=((NDP * ROWS_THREE, 128), F32),
    red_a3=((NDP, ROWS_THREE, 128), F32),
    part3=((NX, ROWS_THREE // NX, 128), F32),
    red_b3=((NX, ROWS_THREE // NX, 128), F32),
    red_c3=((NZ, ROWS_THREE // NX, 128), F32),
    whole3=((NX, ROWS_THREE // NX, 128), F32),
)
PAIRS = dict(
    quad_sems=(4,),
    pix_sems=(2,),
    cot_sems=(NROWS,),
    line_sems=(NX,),
    edge_sems=(2,),
    out_sems=(NX,),
    feat_sems=(NROWS,),
    sems2=(5, NDP),
    sems3=(5, NDP),
)
INPUTS = (
    "pix", "k2", "b2", "gain", "k3", "b3", "db", "weight", "cot", "heights", "widths", "owners"
)
OUTPUTS = ("features", "pixel_grad", "total2", "total3")


def whole_kernel(*refs):
    names = INPUTS + OUTPUTS + tuple(COMPUTE_SCRATCH) + tuple(COMM_SCRATCH)
    r = SimpleNamespace(**dict(zip(names, refs)))
    rest = refs[len(names) :]
    for k, name in enumerate(PAIRS):
        setattr(r, name, (rest[2 * k], rest[2 * k + 1]))
    r.wsend, r.wrecv = rest[2 * len(PAIRS) :]

    c = Comm()
    c.greet()
    load_parameters(r)
    make_tables(c, r)
    pack_cotangent(r)
    spread_taps(r)
    for group in range(4):
        load_pixels(r, r.pix[group * 128 : group * 128 + 128, :], group + 1)
    c.met()
    quad = regroup_quad(c, r)
    next(quad)
    halo = pixel_halo(c, r)
    next(quad, None)
    weights = Drive(*[gather_part(c, r, part) for part in range(len(PARTS))])
    weights.step()
    cot = Drive(bring_cotangent(c, r))
    cot.step()
    r.sums2[...] = jnp.zeros((NDP * ROWS_TWO, 128), F32)
    r.sums3[...] = jnp.zeros((NDP * ROWS_THREE, 128), F32)
    wait_all(halo)
    load_pixels(r, r.pix_left[...], 0)
    load_pixels(r, r.pix_right[...], 5)
    weights.step()
    for ch in range(6):
        forward_two(r, ch)
        if ch == 4:
            weights.step()
    norm_two(r, 0, 16)
    weights.step()
    cot.step()
    weights.step()
    cot.step()
    weights.step()
    cot.finish()
    place_cotangent(r)
    backward_three(r)
    weights.finish()
    for n in range(4):
        project(r, n)
    forward_three(r)
    pack_features(r)
    feat = Drive(take_features(c, r))
    feat.step()
    kernel_three(r, 0, 12)
    sums = Drive(reduce_sums(c, r, "3"))
    sums.step()
    for ab in range(2):
        project_back(r, ab)
    feat.step()
    for ab in range(2, 4):
        project_back(r, ab)
    norm_back(r)
    sums.step()
    kernel_two(r, 0, 4)
    sums.step()
    kernel_two(r, 4, 6)
    last = Drive(reduce_sums(c, r, "2"))
    last.step()
    backward_two(r, 0, 4)
    last.step()
    sums.step()
    backward_two(r, 4, 6)
    store_pixel_grad(r)
    last.step()
    sums.step()
    last.step()
    feat.finish()
    last.finish()
    sums.finish()


def run_kernel(*arrays):
    vmem = pl.BlockSpec(memory_space=pltpu.VMEM)
    scratch = [pltpu.VMEM(*v) for v in COMPUTE_SCRATCH.values()]
    scratch += [pltpu.VMEM(*v) for v in COMM_SCRATCH.values()]
    for shape in PAIRS.values():
        scratch += [pltpu.SemaphoreType.DMA(shape)] * 2
    scratch += [pltpu.SemaphoreType.DMA((len(PARTS), 40))] * 2
    return pl.pallas_call(
        whole_kernel,
        out_shape=(
            jax.ShapeDtypeStruct((64, 4, 1536), BF16),
            jax.ShapeDtypeStruct((512, 768), BF16),
            jax.ShapeDtypeStruct((NDP, ROWS_TWO, 128), F32),
            jax.ShapeDtypeStruct((NDP, ROWS_THREE, 128), F32),
        ),
        in_specs=[vmem] * len(INPUTS),
        out_specs=(vmem,) * 4,
        scratch_shapes=scratch,
        compiler_params=pltpu.CompilerParams(
            collective_id=0, has_side_effects=True, vmem_limit_bytes=60 * 1024 * 1024
        ),
    )(*arrays)


def body(
    pixels,
    kernel_two,
    bias_two,
    gain_two,
    down_weight,
    down_bias,
    kernel_three,
    bias_three,
    cotangent,
    tile_height,
    tile_width,
    tile_owner,
):
    features, pixel_grad, total2, total3 = run_kernel(
        pixels.reshape(512, 768),
        kernel_two,
        bias_two,
        gain_two,
        kernel_three,
        bias_three,
        down_bias,
        down_weight,
        cotangent[0].reshape(256, 1536),
        tile_height,
        tile_width,
        tile_owner,
    )
    factor = 1.0 / math.sqrt(NROWS * NDP * 64 * 8)
    two = total2.reshape(NDP * ROWS_TWO, 128)[:306].reshape(6, 51, 128) * factor
    two = two.transpose(1, 0, 2).reshape(51, 768)
    three = total3.reshape(NDP * ROWS_THREE, 128)[:600].reshape(12, 50, 128) * factor
    three = three.transpose(1, 0, 2).reshape(50, 1536)
    return (
        features.reshape(1, 64, 4, 1536),
        pixel_grad.reshape(1, 64, 8, 768),
        two[:49],
        two[49],
        two[50],
        three[:49],
        three[49],
    )


def solution(mesh):
    in_specs = (
        P("dp", "rows", None, None),
        P(),
        P(),
        P(),
        P(("rows", "dp"), None),
        P(),
        P(),
        P(),
        P("dp", "rows", None, None),
        P("dp", None),
        P("dp", None),
        P("dp", None),
    )
    out_specs = (P("dp", "rows", None, None), P("dp", "rows", None, None), P(), P(), P(), P(), P())
    return jax.shard_map(body, mesh=mesh, in_specs=in_specs, out_specs=out_specs, check_vma=False)
```

```python
import functools
import math
from types import SimpleNamespace

import jax
import jax.numpy as jnp
from jax import lax
from jax.experimental import pallas as pl
from jax.experimental.pallas import tpu as pltpu
from jax.sharding import PartitionSpec as P

MESH = pl.DeviceIdType.MESH
F32 = jnp.float32
BF16 = jnp.bfloat16
epsilon = 1e-06

NZ, NX, NY = 8, 4, 4
NROWS = NZ * NX
NDP = 2 * NY
SIZE = {"x": NX, "y": NY, "z": NZ}
PARTS = ((0, 0, 384, "zxy"), (1, 0, 384, "zyx"), (2, 0, 384, "zxy"))
WIN = 56
OWN = 12
BASE = 8
ROWS_TWO = 40
ROWS_THREE = 96


def iota_of(shape, dim):
    return lax.broadcasted_iota(jnp.int32, shape, dim)


def as_row(column):
    n = column.shape[0]
    eye = iota_of((n, n), 0) == iota_of((n, n), 1)
    return jnp.sum(jnp.where(eye, column, 0.0), axis=0, keepdims=True)


def as_column(row):
    n = row.shape[1]
    eye = iota_of((n, n), 0) == iota_of((n, n), 1)
    return jnp.sum(jnp.where(eye, row, 0.0), axis=1, keepdims=True)


def make_tables(c, r):
    n = r.heights.shape[1]
    heights, widths, owners = (
        ref[...].astype(F32) for ref in (r.heights, r.widths, r.owners)
    )
    before, after = iota_of((n, n), 0), iota_of((n, n), 1)
    lengths = jnp.broadcast_to(heights, (16, n)).astype(BF16)
    ends = jnp.dot(lengths, one_hot(before <= after), preferred_element_type=F32)[0:1]
    starts = ends - heights
    earlier = one_hot((as_column(owners) == owners) & (before < after))
    own_start = jnp.dot(lengths, earlier, preferred_element_type=F32)[0:1]

    def add(hits, table):
        return jnp.sum(jnp.where(hits, table, 0.0), axis=1, keepdims=True)

    row = (c.rows * 32 - OWN + iota_of((WIN, n), 0)).astype(F32)
    hits = (starts <= row) & (row < ends)
    tile = add(hits, (iota_of((WIN, n), 1) + 1).astype(F32))
    width = jnp.broadcast_to(add(hits, widths), (WIN, 128))
    r.tile[...] = jnp.zeros((WIN + 16, 128), F32)
    r.tile[8 : 8 + WIN, :] = jnp.broadcast_to(tile, (WIN, 128))
    here = r.tile[8 : 8 + WIN, :]
    for k in range(7):
        there = r.tile[5 + k : 5 + k + WIN, :]
        r.masks[k] = jnp.where(there == here, 1.0, 0.0)
    for q in range(4):
        r.masks[7 + q] = jnp.where(width > 2.0 * q, 1.0, 0.0)
    z, x = c.pos["z"], c.pos["x"]
    line = iota_of((256, n), 0)
    strip = z * 128 + x + 4 * (line // 8)
    hits = (starts <= strip.astype(F32)) & (strip.astype(F32) < ends)
    line = iota_of((256, 1), 0)
    strip = z * 128 + x + 4 * (line // 8)
    at = (add(hits, owners).astype(jnp.int32) * 2 + strip // 64 % 2) * 8 + line % 8
    r.strip_col[...] = at
    r.strip_row[...] = as_row(at.astype(F32)).astype(jnp.int32)
    own = (iota_of((256, n), 0) // 4).astype(F32)
    hits = (owners == c.rows.astype(F32)) & (own_start <= own) & (own < own_start + heights)
    row = add(hits, starts - own_start).astype(jnp.int32) + line // 4
    at = ((row // 128 * NX + row % 4) * 2 + row // 64 % 2) * 8 + 2 * (line % 4)
    at = jnp.where(add(hits, 1.0) > 0.0, at, -1024)
    r.own_col[...] = at
    r.own_row[...] = as_row(at.astype(F32)).astype(jnp.int32)


def load_parameters(r):
    r.par2[0:49, :] = r.k2[...]
    r.par2[49:50, :] = r.b2[...].reshape(1, 768)
    r.par2[50:51, :] = r.gain[...].reshape(1, 768)
    r.par3[0:49, :] = r.k3[...]
    r.par3[49:50, :] = r.b3[...].reshape(1, 1536)
    r.par3[50:51, :] = r.db[...].reshape(1, 1536)


def load_weights(r):
    r.wpart[...] = jnp.zeros((4, 16, 384), BF16)
    for k in range(4):
        r.wpart[k, 0:12, :] = r.weight[:, k * 384 : k * 384 + 384]


def spread_taps(r):
    def one(t, _):
        row = r.par2[pl.ds(t, 1), :]
        for ch in range(6):
            r.kb2[ch, t] = jnp.broadcast_to(row[:, ch * 128 : ch * 128 + 128], (8, 128))
        row = r.par3[pl.ds(t, 1), :]
        for ch in range(12):
            r.kb3[ch, t] = jnp.broadcast_to(row[:, ch * 128 : ch * 128 + 128], (8, 128))
        return 0

    lax.fori_loop(0, 50, one, 0)


def iotas(rows, cols):
    return (
        lax.broadcasted_iota(jnp.int32, (rows, cols), 0),
        lax.broadcasted_iota(jnp.int32, (rows, cols), 1),
    )


def one_hot(hit):
    return jnp.where(hit, 1.0, 0.0).astype(BF16)


def turn(back):
    row, col = iotas(128, 128)
    if back:
        row, col = col, row
    ac = row // 8
    return one_hot(col == (2 * (row % 8) + ac // 8) * 8 + ac % 8)


def load_pixels(r, lines, group):
    block = jnp.dot(turn(False), lines, preferred_element_type=F32)
    s0 = 4 + 8 * group
    for ac in range(16):
        inside = r.masks[7 + (ac % 8) // 2, s0 : s0 + 8, :]
        for ch in range(6):
            part = block[ac * 8 : ac * 8 + 8, ch * 128 : ch * 128 + 128]
            r.x[ch, ac, s0 : s0 + 8, :] = part * inside


def conv2(r, src, ch, a, s0, flip, accs):
    for i in range(7):
        t = a + i - 3
        par, shift = t % 2, t // 2
        cols = [src[ch, par * 8 + c, pl.ds(s0 + shift, 8), :] for c in range(8)]
        if shift != 0:
            same = r.masks[shift + 3, pl.ds(s0, 8), :]
            cols = [v * same for v in cols]
        for j in range(7):
            tap = 7 * i + j
            k = r.kb2[ch, 48 - tap if flip else tap]
            for c in range(8):
                if 0 <= c + j - 3 < 8:
                    term = cols[c + j - 3] * k
                    accs[c] = term if accs[c] is None else accs[c] + term
    return accs


def conv3(r, src, ch, s0, flip, accs):
    for i in range(7):
        cols = [src[ch, q, pl.ds(s0 + i - 3, 8), :] for q in range(4)]
        if i != 3:
            same = r.masks[i, pl.ds(s0, 8), :]
            cols = [v * same for v in cols]
        for j in range(7):
            tap = 7 * i + j
            k = r.kb3[ch, 48 - tap if flip else tap]
            for q in range(4):
                if 0 <= q + j - 3 < 4:
                    term = cols[q + j - 3] * k
                    accs[q] = term if accs[q] is None else accs[q] + term
    return accs


def forward_two(r, ch):
    def block(b, _):
        s0 = BASE + 8 * b
        for a in range(2):
            accs = conv2(r, r.x, ch, a, s0, False, [r.kb2[ch, 49]] * 8)
            for c in range(8):
                r.act[ch, a * 8 + c, pl.ds(8 * b, 8), :] = accs[c]
        return 0

    lax.fori_loop(0, 5, block, 0)


def channel_mean(parts):
    total = parts[0]
    for v in parts[1:]:
        total = total + v
    return jnp.sum(total, axis=1, keepdims=True) * (1.0 / 768)


def norm_two(r, low, high):
    def one(ac, _):
        a, col = ac // 8, ac % 8
        q, b2 = col // 2, col % 2
        for b in range(5):
            inside = r.masks[7 + q, pl.ds(BASE + 8 * b, 8), :]
            act = [r.act[ch, ac, 8 * b : 8 * b + 8, :] * inside for ch in range(6)]
            mean = channel_mean(act)
            act = [v - mean for v in act]
            inverse = lax.rsqrt(channel_mean([v * v for v in act]) + epsilon)
            r.inv[ac, 8 * b : 8 * b + 8, :] = jnp.broadcast_to(inverse, (8, 128))
            for ch in range(6):
                nhat = act[ch] * inverse
                r.act[ch, ac, 8 * b : 8 * b + 8, :] = nhat
                gain = r.par2[50:51, ch * 128 : ch * 128 + 128]
                r.lhs[a * 2 + b2, pl.ds(q * 40 + 8 * b, 8), ch * 128 : ch * 128 + 128] = nhat * gain
        return 0

    lax.fori_loop(low, high, one, 0)


def weight_panel(r, n, ab):
    return r.w[n // 2, n % 2, pl.ds(2 * ab, 2)].reshape(768, 384)


def project(r, n):
    total = jnp.zeros((160, 384), F32)
    for ab in range(4):
        total = total + jnp.dot(
            r.lhs[ab].astype(BF16), weight_panel(r, n, ab), preferred_element_type=F32
        )
    for cb in range(3):
        ch = n * 3 + cb
        bias = r.par3[50:51, ch * 128 : ch * 128 + 128]
        for q in range(4):
            part = total[q * 40 : q * 40 + 40, cb * 128 : cb * 128 + 128] + bias
            part = part * r.masks[7 + q, BASE : BASE + 40, :]
            r.down[ch, q, BASE : BASE + 40, :] = part.astype(BF16).astype(F32)


def forward_three(r):
    def one(ch, _):
        for b in range(4):
            s0 = OWN + 8 * b
            accs = conv3(r, r.down, ch, s0, False, [r.kb3[ch, 49]] * 4)
            for q in range(4):
                inside = r.masks[7 + q, s0 : s0 + 8, :]
                out = r.down[ch, q, s0 : s0 + 8, :] + accs[q] * inside
                r.feat[ch, q * 32 + 8 * b : q * 32 + 8 * b + 8, :] = out
        return 0

    lax.fori_loop(0, 12, one, 0)


def pack_features(r):
    row, col = iotas(256, 128)
    at = (row // 2 % 4) * 32 + (row // 8 % 8) * 4 + row // 64
    total = jnp.zeros((256, 768), F32)
    for half in range(2):
        pick = one_hot((col == at) & (row % 2 == half))
        part = jnp.concatenate(
            [r.feat[half * 6 + k].astype(BF16) for k in range(6)], axis=1
        )
        total = total + jnp.dot(pick, part, preferred_element_type=F32)
    r.feat_out[...] = total.astype(BF16).reshape(4, 64, 768)


def place_cotangent(r):
    row, col = iotas(4 * WIN, 384)
    own = col - 64
    edge = (col % 16 // 8) * 4 + jnp.where(col < 64, col // 16 - 8, (col - 320) // 16 + 32)
    mid = (own % 64 // 8) * 4 + own // 64
    p = jnp.where((col >= 64) & (col < 320), mid, edge)
    line = (col % 8 // 2) * WIN + p + OWN
    lines = jnp.concatenate(
        [r.cot_left[...].reshape(64, 768), r.cot_own[...].reshape(256, 768), r.cot_right[...].reshape(64, 768)],
        axis=0,
    )
    for half in range(2):
        pick = one_hot((row == line) & (col % 2 == half))
        part = jnp.dot(pick, lines, preferred_element_type=F32)
        for k in range(6):
            for q in range(4):
                block = part[q * WIN : q * WIN + WIN, k * 128 : k * 128 + 128]
                r.gout[half * 6 + k, q] = block * r.masks[7 + q]


def backward_three(r):
    def one(ch, _):
        for b in range(5):
            s0 = BASE + 8 * b
            accs = conv3(r, r.gout, ch, s0, True, [None] * 4)
            for q in range(4):
                inside = r.masks[7 + q, s0 : s0 + 8, :]
                out = (r.gout[ch, q, s0 : s0 + 8, :] + accs[q]) * inside
                r.gdown[ch, q * 40 + 8 * b : q * 40 + 8 * b + 8, :] = out
        return 0

    lax.fori_loop(0, 12, one, 0)


def row_sum(v):
    return jnp.sum(v, axis=0, keepdims=True)


def kernel_three(r, low, high):
    def one(ch, _):
        bias = None
        for i in range(7):
            accs = [None] * 7
            for b in range(4):
                s0 = OWN + 8 * b
                grads = [r.gout[ch, q, s0 : s0 + 8, :] for q in range(4)]
                if i == 0:
                    for v in grads:
                        bias = v if bias is None else bias + v
                if i != 3:
                    same = r.masks[i, s0 : s0 + 8, :]
                    grads = [v * same for v in grads]
                field = [r.down[ch, q, s0 + i - 3 : s0 + i + 5, :] for q in range(4)]
                for j in range(7):
                    for q in range(4):
                        if 0 <= q + j - 3 < 4:
                            term = grads[q] * field[q + j - 3]
                            accs[j] = term if accs[j] is None else accs[j] + term
            for j in range(7):
                r.sums3[pl.ds(ch * 50 + 7 * i + j, 1), :] = row_sum(accs[j])
        r.sums3[pl.ds(ch * 50 + 49, 1), :] = row_sum(bias)
        return 0

    lax.fori_loop(low, high, one, 0)


def project_back(r, ab):
    total = jnp.zeros((160, 768), F32)
    for n in range(4):
        part = jnp.concatenate([r.gdown[n * 3 + cb].astype(BF16) for cb in range(3)], axis=1)
        total = total + lax.dot_general(
            part, weight_panel(r, n, ab), (((1,), (1,)), ((), ())), preferred_element_type=F32
        )
    r.lhs[ab] = total.astype(BF16).astype(F32)


def norm_back(r):
    zeros = jnp.zeros((8, 128), F32)

    def one(ac, carry):
        carry = list(carry)
        a, col = ac // 8, ac % 8
        q, b2 = col // 2, col % 2
        row = lax.broadcasted_iota(jnp.int32, (8, 128), 0)
        for b in range(5):
            inside = r.masks[7 + q, pl.ds(BASE + 8 * b, 8), :]
            inverse = r.inv[ac, 8 * b : 8 * b + 8, :] * inside
            nhat = [r.act[ch, ac, 8 * b : 8 * b + 8, :] for ch in range(6)]
            gn = [
                r.lhs[a * 2 + b2, pl.ds(q * 40 + 8 * b, 8), ch * 128 : ch * 128 + 128]
                for ch in range(6)
            ]
            scaled = [gn[ch] * r.par2[50:51, ch * 128 : ch * 128 + 128] for ch in range(6)]
            mean = channel_mean(scaled)
            mixed = channel_mean([s * v for s, v in zip(scaled, nhat)])
            for ch in range(6):
                grad = inverse * (scaled[ch] - mean - nhat[ch] * mixed)
                grad = grad.astype(BF16).astype(F32)
                r.gact[ch, ac, BASE + 8 * b : BASE + 8 * b + 8, :] = grad
                gain_term = gn[ch] * nhat[ch]
                if b in (0, 4):
                    keep = row >= 4 if b == 0 else row < 4
                    gain_term = jnp.where(keep, gain_term, 0.0)
                    grad = jnp.where(keep, grad, 0.0)
                carry[ch] = carry[ch] + grad
                carry[6 + ch] = carry[6 + ch] + gain_term
        return tuple(carry)

    sums = lax.fori_loop(0, 16, one, (zeros,) * 12)
    for ch in range(6):
        r.sums2[ch * 51 + 49 : ch * 51 + 50, :] = row_sum(sums[ch])
        r.sums2[ch * 51 + 50 : ch * 51 + 51, :] = row_sum(sums[6 + ch])


def kernel_two(r, low, high):
    def one(ch, _):
        for i in range(7):
            accs = [None] * 7
            for a in range(2):
                t = a + i - 3
                par, shift = t % 2, t // 2
                for b in range(4):
                    s0 = OWN + 8 * b
                    grads = [r.gact[ch, a * 8 + c, s0 : s0 + 8, :] for c in range(8)]
                    if shift != 0:
                        same = r.masks[shift + 3, s0 : s0 + 8, :]
                        grads = [v * same for v in grads]
                    field = [
                        r.x[ch, par * 8 + c, s0 + shift : s0 + shift + 8, :] for c in range(8)
                    ]
                    for j in range(7):
                        for c in range(8):
                            if 0 <= c + j - 3 < 8:
                                term = grads[c] * field[c + j - 3]
                                accs[j] = term if accs[j] is None else accs[j] + term
            for j in range(7):
                r.sums2[pl.ds(ch * 51 + 7 * i + j, 1), :] = row_sum(accs[j])
        return 0

    lax.fori_loop(low, high, one, 0)


def backward_two(r, low, high):
    def one(ch, _):
        for b in range(4):
            s0 = OWN + 8 * b
            for a in range(2):
                accs = conv2(r, r.gact, ch, a, s0, True, [None] * 8)
                for c in range(8):
                    inside = r.masks[7 + c // 2, s0 : s0 + 8, :]
                    at = (a * 8 + c) * 8
                    r.pgrad[b, ch, at : at + 8, :] = accs[c] * inside
        return 0

    lax.fori_loop(low, high, one, 0)


def store_pixel_grad(r):
    for b in range(4):
        lines = jnp.concatenate([r.pgrad[b, ch].astype(BF16) for ch in range(6)], axis=1)
        out = jnp.dot(turn(True), lines, preferred_element_type=F32)
        r.pixel_grad[b * 128 : b * 128 + 128, :] = out.astype(BF16)


COMPUTE_SCRATCH = dict(
    masks=((11, WIN, 128), F32),
    tile=((WIN + 16, 128), F32),
    par2=((56, 768), F32),
    par3=((56, 1536), F32),
    own_row=((1, 256), jnp.int32),
    own_col=((256, 1), jnp.int32),
    strip_row=((1, 256), jnp.int32),
    strip_col=((256, 1), jnp.int32),
    kb2=((6, 50, 8, 128), F32),
    kb3=((12, 50, 8, 128), F32),
    x=((6, 16, WIN, 128), F32),
    act=((6, 16, 40, 128), F32),
    inv=((16, 40, 128), F32),
    lhs=((4, 160, 768), F32),
    down=((12, 4, WIN, 128), F32),
    feat=((12, 128, 128), F32),
    gout=((12, 4, WIN, 128), F32),
    gdown=((12, 160, 128), F32),
    gact=((6, 16, WIN, 128), F32),
    pgrad=((4, 6, 128, 128), F32),
)


class Comm:
    def __init__(self):
        rows, dp = lax.axis_index("rows"), lax.axis_index("dp")
        self.rows, self.dp = rows, dp
        self.pos = {"z": rows // NX, "x": rows % NX, "y": dp // 2}
        self.core = dp % 2

    def device(self, **moved):
        at = {**self.pos, "core": self.core, **moved}
        return (at["z"] * NX + at["x"], at["y"] * 2 + at["core"])

    def greet(self):
        barrier = pltpu.get_barrier_semaphore()

        def one(k, _):
            peer = (lax.rem(self.rows + k, NROWS), self.dp)
            pl.semaphore_signal(barrier, inc=1, device_id=peer, device_id_type=MESH)
            return 0

        lax.fori_loop(1, NROWS, one, 0)
        for k in range(1, NDP):
            peer = (self.rows, lax.rem(self.dp + k, NDP))
            pl.semaphore_signal(barrier, inc=1, device_id=peer, device_id_type=MESH)

    def met(self):
        pl.semaphore_wait(pltpu.get_barrier_semaphore(), NROWS + NDP - 2)


def remote(src, dst, sems, k, device):
    return pltpu.make_async_remote_copy(
        src_ref=src,
        dst_ref=dst,
        send_sem=sems[0].at[k],
        recv_sem=sems[1].at[k],
        device_id=device,
        device_id_type=MESH,
    )


def wait_all(copies):
    for copy in copies:
        copy.wait()


def regroup_quad(c, r):
    quad, m = c.dp // 4 * 4, c.dp % 4
    copies = []
    for k in range(1, 4):
        other = lax.rem(m + k, 4)
        copy = remote(r.wpart.at[other], r.wquad.at[m], r.quad_sems, k, (c.rows, quad + other))
        copy.start()
        copies.append(copy)
    r.wquad[m] = r.wpart[m]
    yield
    wait_all(copies)
    row, col = iotas(48, 64)
    pick = one_hot((col // 16 * 12 + col % 16 == row) & (col % 16 < 12))
    block = jnp.dot(pick, r.wquad[...].reshape(64, 384), preferred_element_type=F32).astype(BF16)
    y = c.pos["y"]
    for j in range(3):
        r.w[y % 2, c.core, c.pos["z"], c.pos["x"], y // 2, j] = block[j * 16 : j * 16 + 16]


def gather_part(c, r, part):
    sub, lane, lanes, order = PARTS[part]
    sems = (r.wsend.at[part], r.wrecv.at[part])
    sent = []

    def block(core, whole, cut=slice(None), **at):
        at = {**c.pos, **at}
        z = cut if "z" in whole else at["z"]
        x = at["x"] if "x" not in whole else slice(None) if "z" in whole else cut
        yl, yh = (slice(None), slice(None)) if "y" in whole else (at["y"] % 2, at["y"] // 2)
        return r.w.at[yl, core, z, x, yh, sub, :, pl.ds(lane, lanes)]

    def push(mine, device):
        copy = remote(mine, mine, sems, len(sent), device)
        copy.start()
        sent.append(copy)
        return len(sent) - 1

    def arrived(k, got):
        remote(got, got, sems, k, c.device(core=1 - c.core)).wait_recv()

    for level in range(2):
        axis, whole = order[level], order[:level]
        n, here = SIZE[axis], c.pos[axis]
        slots = [
            push(block(c.core, whole), c.device(**{axis: lax.rem(here + k, n)})) for k in range(1, n)
        ]
        yield
        for k, slot in enumerate(slots):
            arrived(slot, block(c.core, whole, **{axis: lax.rem(here + n - 1 - k, n)}))
    axis, whole = order[2], order[:2]
    here, n = c.pos[axis], SIZE[axis]
    way = 1 - 2 * c.core
    sibling = c.device(core=1 - c.core)
    half = (NZ if "z" in whole else NX) // 2
    cuts = [pl.ds(0, half), pl.ds(half, half)]
    family = []

    def at(step):
        return {axis: lax.rem(here + step + 2 * n, n)}

    def mine(step, cut):
        return block(c.core, whole, cut, **at(step))

    def send(step, ahead, cut):
        return push(mine(step, cut), c.device(**at(ahead)))

    def share(step, cut):
        family.append((push(mine(step, cut), sibling), -step, cut))

    moving = {}
    for k, cut in enumerate(cuts):
        moving[k] = (send(0, way, cut), send(0, -way, cut))
    for cut in cuts:
        share(0, cut)
    for step in range(1, n // 2 + 1):
        for k, cut in enumerate(cuts):
            yield
            if step == n // 2:
                arrived(moving[k], mine(step, cut))
                family.append((push(mine(step, cut), sibling), step, cut))
                continue
            ahead, back = moving[k]
            arrived(ahead, mine(-way * step, cut))
            if step == n // 2 - 1:
                moving[k] = send(-way * step, way, cut)
            else:
                again = send(-way * step, way, cut)
            share(-way * step, cut)
            arrived(back, mine(way * step, cut))
            if step < n // 2 - 1:
                moving[k] = (again, send(way * step, -way, cut))
            share(way * step, cut)
    yield
    for slot, step, cut in family:
        arrived(slot, block(1 - c.core, whole, cut, **at(step)))
    for copy in sent:
        copy.wait_send()


def exchange_start(c, src, dst, sems):
    def one(k, _):
        peer = lax.rem(c.rows + k, NROWS)
        remote(
            src.at[pl.ds(peer * 16, 16)], dst.at[pl.ds(c.rows * 16, 16)], sems, k, (peer, c.dp)
        ).start()
        return 0

    lax.fori_loop(1, NROWS, one, 0)
    mine = pl.ds(pl.multiple_of(c.rows * 16, 16), 16)
    dst[mine] = src[mine]


def exchange_wait(c, src, dst, sems):
    def one(k, _):
        peer = lax.rem(c.rows - k + NROWS, NROWS)
        remote(
            src.at[pl.ds(peer * 16, 16)], dst.at[pl.ds(peer * 16, 16)], sems, k, (peer, c.dp)
        ).wait()
        return 0

    lax.fori_loop(1, NROWS, one, 0)


def to_all(n, here, src_of, dst, sems, device_of):
    copies = []
    for k in range(1, n):
        other = lax.rem(here + k, n)
        copy = remote(src_of(other), dst.at[here], sems, k, device_of(other))
        copy.start()
        copies.append(copy)
    return copies


def neighbours(c):
    return (
        (lax.rem(c.rows + NROWS - 1, NROWS), c.dp),
        (lax.rem(c.rows + 1, NROWS), c.dp),
    )


def pixel_halo(c, r):
    left, right = neighbours(c)
    copies = [
        remote(r.pix.at[pl.ds(0, 80)], r.pix_right.at[pl.ds(0, 80)], r.pix_sems, 0, left),
        remote(r.pix.at[pl.ds(432, 80)], r.pix_left.at[pl.ds(48, 80)], r.pix_sems, 1, right),
    ]
    for copy in copies:
        copy.start()
    r.pix_left[0:48] = jnp.zeros((48, 768), BF16)
    r.pix_right[80:128] = jnp.zeros((48, 768), BF16)
    return copies


def pack_cotangent(r):
    row, _ = iotas(512, 256)
    total = jnp.zeros((512, 768), F32)
    for half in range(2):
        pick = one_hot(row == r.own_row[...] + half)
        lines = r.cot[:, :, half * 768 : half * 768 + 768].astype(F32).reshape(256, 768)
        total = total + jnp.dot(pick, lines.astype(BF16), preferred_element_type=F32)
    r.cot_send[...] = total.astype(BF16)


def bring_cotangent(c, r):
    x = c.pos["x"]
    exchange_start(c, r.cot_send, r.cot_recv, r.cot_sems)
    yield
    exchange_wait(c, r.cot_send, r.cot_recv, r.cot_sems)
    _, col = iotas(256, 512)
    pick = one_hot(col == r.strip_col[...])
    lines = jnp.dot(pick, r.cot_recv[...], preferred_element_type=F32).astype(BF16)
    r.cot_mid[...] = lines.reshape(4, 64, 768)
    copies = to_all(
        NX, x, lambda o: r.cot_mid.at[o], r.cot_own, r.line_sems, lambda o: c.device(x=o)
    )
    r.cot_own[x] = r.cot_mid[x]
    yield
    wait_all(copies)
    left, right = neighbours(c)
    copies = [
        remote(r.cot_own.at[:, pl.ds(0, 16)], r.cot_right, r.edge_sems, 0, left),
        remote(r.cot_own.at[:, pl.ds(48, 16)], r.cot_left, r.edge_sems, 1, right),
    ]
    for copy in copies:
        copy.start()
    yield
    wait_all(copies)


def take_features(c, r):
    x = c.pos["x"]
    copies = to_all(
        NX, x, lambda o: r.feat_out.at[o], r.feat_mid, r.out_sems, lambda o: c.device(x=o)
    )
    r.feat_mid[x] = r.feat_out[x]
    yield
    wait_all(copies)
    row, _ = iotas(512, 256)
    pick = one_hot(row == r.strip_row[...])
    r.feat_send[...] = jnp.dot(
        pick, r.feat_mid[...].reshape(256, 768), preferred_element_type=F32
    ).astype(BF16)
    exchange_start(c, r.feat_send, r.feat_recv, r.feat_sems)
    yield
    exchange_wait(c, r.feat_send, r.feat_recv, r.feat_sems)
    _, col = iotas(256, 512)
    for half in range(2):
        pick = one_hot(col == r.own_col[...] + half)
        lines = jnp.dot(pick, r.feat_recv[...], preferred_element_type=F32)
        r.features[:, :, half * 768 : half * 768 + 768] = lines.reshape(64, 4, 768).astype(BF16)


def total_of(ref, n):
    total = ref[0]
    for k in range(1, n):
        total = total + ref[k]
    return total


def reduce_sums(c, r, which):
    sums, red_a, red_b, red_c, out, sems = (
        getattr(r, name + which) for name in ("sums", "red_a", "red_b", "red_c", "total", "sems")
    )
    x, z = c.pos["x"], c.pos["z"]
    size = sums.shape[0] // NDP
    split = red_b.shape[1] < size

    def family(k):
        return (sems[0].at[k], sems[1].at[k])

    def dp_device(other):
        return (c.rows, other)

    def x_device(other):
        return c.device(x=other)

    blocks = sums.reshape(NDP, size, 128)
    copies = to_all(NDP, c.dp, lambda o: blocks.at[o], red_a, family(0), dp_device)
    red_a[c.dp] = sums[pl.ds(pl.multiple_of(c.dp * size, 8), size), :]
    yield
    wait_all(copies)
    if split:
        r.part3[...] = total_of(red_a, NDP).reshape(NX, size // NX, 128)
        copies = to_all(NX, x, lambda o: r.part3.at[o], red_b, family(1), x_device)
        red_b[x] = r.part3[x]
    else:
        red_b[x] = total_of(red_a, NDP)
        copies = to_all(NX, x, lambda o: red_b.at[x], red_b, family(1), x_device)
    yield
    wait_all(copies)
    red_c[z] = total_of(red_b, NX)
    copies = to_all(NZ, z, lambda o: red_c.at[z], red_c, family(2), lambda o: c.device(z=o))
    yield
    wait_all(copies)
    if split:
        r.whole3[x] = total_of(red_c, NZ)
        copies = to_all(NX, x, lambda o: r.whole3.at[x], r.whole3, family(4), x_device)
        yield
        wait_all(copies)
        out[c.dp] = r.whole3[...].reshape(size, 128)
    else:
        out[c.dp] = total_of(red_c, NZ)
    copies = to_all(NDP, c.dp, lambda o: out.at[c.dp], out, family(3), dp_device)
    yield
    wait_all(copies)


class Drive:
    def __init__(self, *tasks):
        self.tasks = list(tasks)

    def step(self):
        for task in list(self.tasks):
            if next(task, "end") == "end":
                self.tasks.remove(task)

    def finish(self):
        while self.tasks:
            self.step()


COMM_SCRATCH = dict(
    w=((2, 2, NZ, NX, 2, 3, 16, 384), BF16),
    wpart=((4, 16, 384), BF16),
    wquad=((4, 16, 384), BF16),
    pix_left=((128, 768), BF16),
    pix_right=((128, 768), BF16),
    cot_send=((NROWS * 16, 768), BF16),
    cot_recv=((NROWS * 16, 768), BF16),
    cot_mid=((4, 64, 768), BF16),
    cot_own=((4, 64, 768), BF16),
    cot_left=((4, 16, 768), BF16),
    cot_right=((4, 16, 768), BF16),
    feat_out=((4, 64, 768), BF16),
    feat_mid=((4, 64, 768), BF16),
    feat_send=((NROWS * 16, 768), BF16),
    feat_recv=((NROWS * 16, 768), BF16),
    sums2=((NDP * ROWS_TWO, 128), F32),
    red_a2=((NDP, ROWS_TWO, 128), F32),
    red_b2=((NX, ROWS_TWO, 128), F32),
    red_c2=((NZ, ROWS_TWO, 128), F32),
    sums3=((NDP * ROWS_THREE, 128), F32),
    red_a3=((NDP, ROWS_THREE, 128), F32),
    part3=((NX, ROWS_THREE // NX, 128), F32),
    red_b3=((NX, ROWS_THREE // NX, 128), F32),
    red_c3=((NZ, ROWS_THREE // NX, 128), F32),
    whole3=((NX, ROWS_THREE // NX, 128), F32),
)
PAIRS = dict(
    quad_sems=(4,),
    pix_sems=(2,),
    cot_sems=(NROWS,),
    line_sems=(NX,),
    edge_sems=(2,),
    out_sems=(NX,),
    feat_sems=(NROWS,),
    sems2=(5, NDP),
    sems3=(5, NDP),
)
INPUTS = (
    "pix", "k2", "b2", "gain", "k3", "b3", "db", "weight", "cot", "heights", "widths", "owners"
)
OUTPUTS = ("features", "pixel_grad", "total2", "total3")


def whole_kernel(*refs):
    names = INPUTS + OUTPUTS + tuple(COMPUTE_SCRATCH) + tuple(COMM_SCRATCH)
    r = SimpleNamespace(**dict(zip(names, refs)))
    rest = refs[len(names) :]
    for k, name in enumerate(PAIRS):
        setattr(r, name, (rest[2 * k], rest[2 * k + 1]))
    r.wsend, r.wrecv = rest[2 * len(PAIRS) :]

    c = Comm()
    c.greet()
    load_weights(r)
    c.met()
    quad = regroup_quad(c, r)
    next(quad)
    halo = pixel_halo(c, r)
    make_tables(c, r)
    next(quad, None)
    weights = Drive(*[gather_part(c, r, part) for part in range(len(PARTS))])
    weights.step()
    load_parameters(r)
    spread_taps(r)
    for group in range(4):
        load_pixels(r, r.pix[group * 128 : group * 128 + 128, :], group + 1)
    pack_cotangent(r)
    wait_all(halo)
    load_pixels(r, r.pix_left[...], 0)
    load_pixels(r, r.pix_right[...], 5)
    weights.step()
    cot = Drive(bring_cotangent(c, r))
    cot.step()
    r.sums2[...] = jnp.zeros((NDP * ROWS_TWO, 128), F32)
    r.sums3[...] = jnp.zeros((NDP * ROWS_THREE, 128), F32)
    for ch in range(6):
        forward_two(r, ch)
        if ch == 4:
            weights.step()
    norm_two(r, 0, 16)
    weights.step()
    cot.step()
    weights.step()
    cot.step()
    weights.finish()
    for n in range(4):
        project(r, n)
    forward_three(r)
    pack_features(r)
    feat = Drive(take_features(c, r))
    feat.step()
    cot.finish()
    place_cotangent(r)
    backward_three(r)
    feat.step()
    kernel_three(r, 0, 12)
    sums = Drive(reduce_sums(c, r, "3"))
    sums.step()
    for ab in range(4):
        project_back(r, ab)
    norm_back(r)
    kernel_two(r, 0, 3)
    sums.step()
    kernel_two(r, 3, 6)
    last = Drive(reduce_sums(c, r, "2"))
    last.step()
    backward_two(r, 0, 4)
    sums.step()
    last.step()
    backward_two(r, 4, 6)
    store_pixel_grad(r)
    last.step()
    sums.step()
    feat.finish()
    last.step()
    sums.step()
    last.finish()
    sums.finish()


def run_kernel(*arrays):
    vmem = pl.BlockSpec(memory_space=pltpu.VMEM)
    scratch = [pltpu.VMEM(*v) for v in COMPUTE_SCRATCH.values()]
    scratch += [pltpu.VMEM(*v) for v in COMM_SCRATCH.values()]
    for shape in PAIRS.values():
        scratch += [pltpu.SemaphoreType.DMA(shape)] * 2
    scratch += [pltpu.SemaphoreType.DMA((len(PARTS), 40))] * 2
    return pl.pallas_call(
        whole_kernel,
        out_shape=(
            jax.ShapeDtypeStruct((64, 4, 1536), BF16),
            jax.ShapeDtypeStruct((512, 768), BF16),
            jax.ShapeDtypeStruct((NDP, ROWS_TWO, 128), F32),
            jax.ShapeDtypeStruct((NDP, ROWS_THREE, 128), F32),
        ),
        in_specs=[vmem] * len(INPUTS),
        out_specs=(vmem,) * 4,
        scratch_shapes=scratch,
        compiler_params=pltpu.CompilerParams(
            collective_id=0, has_side_effects=True, vmem_limit_bytes=60 * 1024 * 1024
        ),
    )(*arrays)


def body(
    pixels,
    kernel_two,
    bias_two,
    gain_two,
    down_weight,
    down_bias,
    kernel_three,
    bias_three,
    cotangent,
    tile_height,
    tile_width,
    tile_owner,
):
    features, pixel_grad, total2, total3 = run_kernel(
        pixels.reshape(512, 768),
        kernel_two,
        bias_two,
        gain_two,
        kernel_three,
        bias_three,
        down_bias,
        down_weight,
        cotangent[0],
        tile_height,
        tile_width,
        tile_owner,
    )
    factor = 1.0 / math.sqrt(NROWS * NDP * 64 * 8)
    two = total2.reshape(NDP * ROWS_TWO, 128)[:306].reshape(6, 51, 128) * factor
    two = two.transpose(1, 0, 2).reshape(51, 768)
    three = total3.reshape(NDP * ROWS_THREE, 128)[:600].reshape(12, 50, 128) * factor
    three = three.transpose(1, 0, 2).reshape(50, 1536)
    return (
        features.reshape(1, 64, 4, 1536),
        pixel_grad.reshape(1, 64, 8, 768),
        two[:49],
        two[49],
        two[50],
        three[:49],
        three[49],
    )


def solution(mesh):
    in_specs = (
        P("dp", "rows", None, None),
        P(),
        P(),
        P(),
        P(("rows", "dp"), None),
        P(),
        P(),
        P(),
        P("dp", "rows", None, None),
        P("dp", None),
        P("dp", None),
        P("dp", None),
    )
    out_specs = (P("dp", "rows", None, None), P("dp", "rows", None, None), P(), P(), P(), P(), P())
    return jax.shard_map(body, mesh=mesh, in_specs=in_specs, out_specs=out_specs, check_vma=False)
```

```python
import functools
import math
from types import SimpleNamespace

import jax
import jax.numpy as jnp
from jax import lax
from jax.experimental import pallas as pl
from jax.experimental.pallas import tpu as pltpu
from jax.sharding import PartitionSpec as P

MESH = pl.DeviceIdType.MESH
F32 = jnp.float32
BF16 = jnp.bfloat16
epsilon = 1e-06

NZ, NX, NY = 8, 4, 4
NROWS = NZ * NX
NDP = 2 * NY
SIZE = {"x": NX, "y": NY, "z": NZ}
PARTS = ((0, 0, 384, "zxy"), (1, 0, 384, "zyx"), (2, 0, 384, "zxy"))
WIN = 56
OWN = 12
BASE = 8
ROWS_TWO = 40
ROWS_THREE = 96


def iota_of(shape, dim):
    return lax.broadcasted_iota(jnp.int32, shape, dim)


def as_row(column):
    n = column.shape[0]
    eye = iota_of((n, n), 0) == iota_of((n, n), 1)
    return jnp.sum(jnp.where(eye, column, 0.0), axis=0, keepdims=True)


def as_column(row):
    n = row.shape[1]
    eye = iota_of((n, n), 0) == iota_of((n, n), 1)
    return jnp.sum(jnp.where(eye, row, 0.0), axis=1, keepdims=True)


def make_tables(c, r):
    n = r.heights.shape[1]
    heights, widths, owners = (
        ref[...].astype(F32) for ref in (r.heights, r.widths, r.owners)
    )
    before, after = iota_of((n, n), 0), iota_of((n, n), 1)
    lengths = jnp.broadcast_to(heights, (16, n)).astype(BF16)
    ends = jnp.dot(lengths, one_hot(before <= after), preferred_element_type=F32)[0:1]
    starts = ends - heights
    earlier = one_hot((as_column(owners) == owners) & (before < after))
    own_start = jnp.dot(lengths, earlier, preferred_element_type=F32)[0:1]

    def add(hits, table):
        return jnp.sum(jnp.where(hits, table, 0.0), axis=1, keepdims=True)

    row = (c.rows * 32 - OWN + iota_of((WIN, n), 0)).astype(F32)
    hits = (starts <= row) & (row < ends)
    tile = add(hits, (iota_of((WIN, n), 1) + 1).astype(F32))
    width = jnp.broadcast_to(add(hits, widths), (WIN, 128))
    r.tile[...] = jnp.zeros((WIN + 16, 128), F32)
    r.tile[8 : 8 + WIN, :] = jnp.broadcast_to(tile, (WIN, 128))
    here = r.tile[8 : 8 + WIN, :]
    for k in range(7):
        there = r.tile[5 + k : 5 + k + WIN, :]
        r.masks[k] = jnp.where(there == here, 1.0, 0.0)
    for q in range(4):
        r.masks[7 + q] = jnp.where(width > 2.0 * q, 1.0, 0.0)
    z, x = c.pos["z"], c.pos["x"]
    line = iota_of((256, n), 0)
    strip = z * 128 + x + 4 * (line // 8)
    hits = (starts <= strip.astype(F32)) & (strip.astype(F32) < ends)
    line = iota_of((256, 1), 0)
    strip = z * 128 + x + 4 * (line // 8)
    at = (add(hits, owners).astype(jnp.int32) * 2 + strip // 64 % 2) * 8 + line % 8
    r.strip_col[...] = at
    r.strip_row[...] = as_row(at.astype(F32)).astype(jnp.int32)
    own = (iota_of((256, n), 0) // 4).astype(F32)
    hits = (owners == c.rows.astype(F32)) & (own_start <= own) & (own < own_start + heights)
    row = add(hits, starts - own_start).astype(jnp.int32) + line // 4
    at = ((row // 128 * NX + row % 4) * 2 + row // 64 % 2) * 8 + 2 * (line % 4)
    at = jnp.where(add(hits, 1.0) > 0.0, at, -1024)
    r.own_col[...] = at
    r.own_row[...] = as_row(at.astype(F32)).astype(jnp.int32)


def load_parameters(r):
    r.par2[0:49, :] = r.k2[...]
    r.par2[49:50, :] = r.b2[...].reshape(1, 768)
    r.par2[50:51, :] = r.gain[...].reshape(1, 768)
    r.par3[0:49, :] = r.k3[...]
    r.par3[49:50, :] = r.b3[...].reshape(1, 1536)
    r.par3[50:51, :] = r.db[...].reshape(1, 1536)


def load_weights(r):
    r.wpart[...] = jnp.zeros((4, 16, 384), BF16)
    for k in range(4):
        r.wpart[k, 0:12, :] = r.weight[:, k * 384 : k * 384 + 384]


def spread_taps(r):
    def one(t, _):
        row = r.par2[pl.ds(t, 1), :]
        for ch in range(6):
            r.kb2[ch, t] = jnp.broadcast_to(row[:, ch * 128 : ch * 128 + 128], (8, 128))
        row = r.par3[pl.ds(t, 1), :]
        for ch in range(12):
            r.kb3[ch, t] = jnp.broadcast_to(row[:, ch * 128 : ch * 128 + 128], (8, 128))
        return 0

    lax.fori_loop(0, 50, one, 0)


def iotas(rows, cols):
    return (
        lax.broadcasted_iota(jnp.int32, (rows, cols), 0),
        lax.broadcasted_iota(jnp.int32, (rows, cols), 1),
    )


def one_hot(hit):
    return jnp.where(hit, 1.0, 0.0).astype(BF16)


def turn(back):
    row, col = iotas(128, 128)
    if back:
        row, col = col, row
    ac = row // 8
    return one_hot(col == (2 * (row % 8) + ac // 8) * 8 + ac % 8)


def load_pixels(r, lines, group):
    block = jnp.dot(turn(False), lines, preferred_element_type=F32)
    s0 = 4 + 8 * group
    for ac in range(16):
        inside = r.masks[7 + (ac % 8) // 2, s0 : s0 + 8, :]
        for ch in range(6):
            part = block[ac * 8 : ac * 8 + 8, ch * 128 : ch * 128 + 128]
            r.x[ch, ac, s0 : s0 + 8, :] = part * inside


def conv2(r, src, ch, a, s0, flip, accs):
    for i in range(7):
        t = a + i - 3
        par, shift = t % 2, t // 2
        cols = [src[ch, par * 8 + c, pl.ds(s0 + shift, 8), :] for c in range(8)]
        if shift != 0:
            same = r.masks[shift + 3, pl.ds(s0, 8), :]
            cols = [v * same for v in cols]
        for j in range(7):
            tap = 7 * i + j
            k = r.kb2[ch, 48 - tap if flip else tap]
            for c in range(8):
                if 0 <= c + j - 3 < 8:
                    term = cols[c + j - 3] * k
                    accs[c] = term if accs[c] is None else accs[c] + term
    return accs


def conv3(r, src, ch, s0, flip, accs):
    for i in range(7):
        cols = [src[ch, q, pl.ds(s0 + i - 3, 8), :] for q in range(4)]
        if i != 3:
            same = r.masks[i, pl.ds(s0, 8), :]
            cols = [v * same for v in cols]
        for j in range(7):
            tap = 7 * i + j
            k = r.kb3[ch, 48 - tap if flip else tap]
            for q in range(4):
                if 0 <= q + j - 3 < 4:
                    term = cols[q + j - 3] * k
                    accs[q] = term if accs[q] is None else accs[q] + term
    return accs


def forward_two(r, ch):
    def block(b, _):
        s0 = BASE + 8 * b
        for a in range(2):
            accs = conv2(r, r.x, ch, a, s0, False, [r.kb2[ch, 49]] * 8)
            for c in range(8):
                r.act[ch, a * 8 + c, pl.ds(8 * b, 8), :] = accs[c]
        return 0

    lax.fori_loop(0, 5, block, 0)


def channel_mean(parts):
    total = parts[0]
    for v in parts[1:]:
        total = total + v
    return jnp.sum(total, axis=1, keepdims=True) * (1.0 / 768)


def norm_two(r, low, high):
    def one(ac, _):
        a, col = ac // 8, ac % 8
        q, b2 = col // 2, col % 2
        for b in range(5):
            inside = r.masks[7 + q, pl.ds(BASE + 8 * b, 8), :]
            act = [r.act[ch, ac, 8 * b : 8 * b + 8, :] * inside for ch in range(6)]
            mean = channel_mean(act)
            act = [v - mean for v in act]
            inverse = lax.rsqrt(channel_mean([v * v for v in act]) + epsilon)
            r.inv[ac, 8 * b : 8 * b + 8, :] = jnp.broadcast_to(inverse, (8, 128))
            for ch in range(6):
                nhat = act[ch] * inverse
                r.act[ch, ac, 8 * b : 8 * b + 8, :] = nhat
                gain = r.par2[50:51, ch * 128 : ch * 128 + 128]
                r.lhs[a * 2 + b2, pl.ds(q * 40 + 8 * b, 8), ch * 128 : ch * 128 + 128] = nhat * gain
        return 0

    lax.fori_loop(low, high, one, 0)


def weight_panel(r, n, ab):
    return r.w[n // 2, n % 2, pl.ds(2 * ab, 2)].reshape(768, 384)


def project(r, n):
    total = jnp.zeros((160, 384), F32)
    for ab in range(4):
        total = total + jnp.dot(
            r.lhs[ab].astype(BF16), weight_panel(r, n, ab), preferred_element_type=F32
        )
    for cb in range(3):
        ch = n * 3 + cb
        bias = r.par3[50:51, ch * 128 : ch * 128 + 128]
        for q in range(4):
            part = total[q * 40 : q * 40 + 40, cb * 128 : cb * 128 + 128] + bias
            part = part * r.masks[7 + q, BASE : BASE + 40, :]
            r.down[ch, q, BASE : BASE + 40, :] = part.astype(BF16).astype(F32)


def forward_three(r):
    def one(ch, _):
        for b in range(4):
            s0 = OWN + 8 * b
            accs = conv3(r, r.down, ch, s0, False, [r.kb3[ch, 49]] * 4)
            for q in range(4):
                inside = r.masks[7 + q, s0 : s0 + 8, :]
                out = r.down[ch, q, s0 : s0 + 8, :] + accs[q] * inside
                r.feat[ch, q * 32 + 8 * b : q * 32 + 8 * b + 8, :] = out
        return 0

    lax.fori_loop(0, 12, one, 0)


def pack_features(r):
    row, col = iotas(256, 128)
    at = (row // 2 % 4) * 32 + (row // 8 % 8) * 4 + row // 64
    total = jnp.zeros((256, 768), F32)
    for half in range(2):
        pick = one_hot((col == at) & (row % 2 == half))
        part = jnp.concatenate(
            [r.feat[half * 6 + k].astype(BF16) for k in range(6)], axis=1
        )
        total = total + jnp.dot(pick, part, preferred_element_type=F32)
    r.feat_out[...] = total.astype(BF16).reshape(4, 64, 768)


def place_cotangent(r):
    row, col = iotas(4 * WIN, 384)
    own = col - 64
    edge = (col % 16 // 8) * 4 + jnp.where(col < 64, col // 16 - 8, (col - 320) // 16 + 32)
    mid = (own % 64 // 8) * 4 + own // 64
    p = jnp.where((col >= 64) & (col < 320), mid, edge)
    line = (col % 8 // 2) * WIN + p + OWN
    lines = jnp.concatenate(
        [r.cot_left[...].reshape(64, 768), r.cot_own[...].reshape(256, 768), r.cot_right[...].reshape(64, 768)],
        axis=0,
    )
    for half in range(2):
        pick = one_hot((row == line) & (col % 2 == half))
        part = jnp.dot(pick, lines, preferred_element_type=F32)
        for k in range(6):
            for q in range(4):
                block = part[q * WIN : q * WIN + WIN, k * 128 : k * 128 + 128]
                r.gout[half * 6 + k, q] = block * r.masks[7 + q]


def backward_three(r):
    def one(ch, _):
        for b in range(5):
            s0 = BASE + 8 * b
            accs = conv3(r, r.gout, ch, s0, True, [None] * 4)
            for q in range(4):
                inside = r.masks[7 + q, s0 : s0 + 8, :]
                out = (r.gout[ch, q, s0 : s0 + 8, :] + accs[q]) * inside
                r.gdown[ch, q * 40 + 8 * b : q * 40 + 8 * b + 8, :] = out
        return 0

    lax.fori_loop(0, 12, one, 0)


def row_sum(v):
    return jnp.sum(v, axis=0, keepdims=True)


def kernel_three(r, low, high):
    def one(ch, _):
        bias = None
        for i in range(7):
            accs = [None] * 7
            for b in range(4):
                s0 = OWN + 8 * b
                grads = [r.gout[ch, q, s0 : s0 + 8, :] for q in range(4)]
                if i == 0:
                    for v in grads:
                        bias = v if bias is None else bias + v
                if i != 3:
                    same = r.masks[i, s0 : s0 + 8, :]
                    grads = [v * same for v in grads]
                field = [r.down[ch, q, s0 + i - 3 : s0 + i + 5, :] for q in range(4)]
                for j in range(7):
                    for q in range(4):
                        if 0 <= q + j - 3 < 4:
                            term = grads[q] * field[q + j - 3]
                            accs[j] = term if accs[j] is None else accs[j] + term
            for j in range(7):
                r.sums3[pl.ds(ch * 50 + 7 * i + j, 1), :] = row_sum(accs[j])
        r.sums3[pl.ds(ch * 50 + 49, 1), :] = row_sum(bias)
        return 0

    lax.fori_loop(low, high, one, 0)


def project_back(r, ab):
    total = jnp.zeros((160, 768), F32)
    for n in range(4):
        part = jnp.concatenate([r.gdown[n * 3 + cb].astype(BF16) for cb in range(3)], axis=1)
        total = total + lax.dot_general(
            part, weight_panel(r, n, ab), (((1,), (1,)), ((), ())), preferred_element_type=F32
        )
    r.lhs[ab] = total.astype(BF16).astype(F32)


def norm_back(r):
    zeros = jnp.zeros((8, 128), F32)

    def one(ac, carry):
        carry = list(carry)
        a, col = ac // 8, ac % 8
        q, b2 = col // 2, col % 2
        row = lax.broadcasted_iota(jnp.int32, (8, 128), 0)
        for b in range(5):
            inside = r.masks[7 + q, pl.ds(BASE + 8 * b, 8), :]
            inverse = r.inv[ac, 8 * b : 8 * b + 8, :] * inside
            nhat = [r.act[ch, ac, 8 * b : 8 * b + 8, :] for ch in range(6)]
            gn = [
                r.lhs[a * 2 + b2, pl.ds(q * 40 + 8 * b, 8), ch * 128 : ch * 128 + 128]
                for ch in range(6)
            ]
            scaled = [gn[ch] * r.par2[50:51, ch * 128 : ch * 128 + 128] for ch in range(6)]
            mean = channel_mean(scaled)
            mixed = channel_mean([s * v for s, v in zip(scaled, nhat)])
            for ch in range(6):
                grad = inverse * (scaled[ch] - mean - nhat[ch] * mixed)
                grad = grad.astype(BF16).astype(F32)
                r.gact[ch, ac, BASE + 8 * b : BASE + 8 * b + 8, :] = grad
                gain_term = gn[ch] * nhat[ch]
                if b in (0, 4):
                    keep = row >= 4 if b == 0 else row < 4
                    gain_term = jnp.where(keep, gain_term, 0.0)
                    grad = jnp.where(keep, grad, 0.0)
                carry[ch] = carry[ch] + grad
                carry[6 + ch] = carry[6 + ch] + gain_term
        return tuple(carry)

    sums = lax.fori_loop(0, 16, one, (zeros,) * 12)
    for ch in range(6):
        r.sums2[ch * 51 + 49 : ch * 51 + 50, :] = row_sum(sums[ch])
        r.sums2[ch * 51 + 50 : ch * 51 + 51, :] = row_sum(sums[6 + ch])


def kernel_two(r, low, high):
    def one(ch, _):
        for i in range(7):
            accs = [None] * 7
            for a in range(2):
                t = a + i - 3
                par, shift = t % 2, t // 2
                for b in range(4):
                    s0 = OWN + 8 * b
                    grads = [r.gact[ch, a * 8 + c, s0 : s0 + 8, :] for c in range(8)]
                    if shift != 0:
                        same = r.masks[shift + 3, s0 : s0 + 8, :]
                        grads = [v * same for v in grads]
                    field = [
                        r.x[ch, par * 8 + c, s0 + shift : s0 + shift + 8, :] for c in range(8)
                    ]
                    for j in range(7):
                        for c in range(8):
                            if 0 <= c + j - 3 < 8:
                                term = grads[c] * field[c + j - 3]
                                accs[j] = term if accs[j] is None else accs[j] + term
            for j in range(7):
                r.sums2[pl.ds(ch * 51 + 7 * i + j, 1), :] = row_sum(accs[j])
        return 0

    lax.fori_loop(low, high, one, 0)


def backward_two(r, low, high):
    def one(ch, _):
        for b in range(4):
            s0 = OWN + 8 * b
            for a in range(2):
                accs = conv2(r, r.gact, ch, a, s0, True, [None] * 8)
                for c in range(8):
                    inside = r.masks[7 + c // 2, s0 : s0 + 8, :]
                    at = (a * 8 + c) * 8
                    r.pgrad[b, ch, at : at + 8, :] = accs[c] * inside
        return 0

    lax.fori_loop(low, high, one, 0)


def store_pixel_grad(r):
    for b in range(4):
        lines = jnp.concatenate([r.pgrad[b, ch].astype(BF16) for ch in range(6)], axis=1)
        out = jnp.dot(turn(True), lines, preferred_element_type=F32)
        r.pixel_grad[b * 128 : b * 128 + 128, :] = out.astype(BF16)


COMPUTE_SCRATCH = dict(
    masks=((11, WIN, 128), F32),
    tile=((WIN + 16, 128), F32),
    par2=((56, 768), F32),
    par3=((56, 1536), F32),
    own_row=((1, 256), jnp.int32),
    own_col=((256, 1), jnp.int32),
    strip_row=((1, 256), jnp.int32),
    strip_col=((256, 1), jnp.int32),
    kb2=((6, 50, 8, 128), F32),
    kb3=((12, 50, 8, 128), F32),
    x=((6, 16, WIN, 128), F32),
    act=((6, 16, 40, 128), F32),
    inv=((16, 40, 128), F32),
    lhs=((4, 160, 768), F32),
    down=((12, 4, WIN, 128), F32),
    feat=((12, 128, 128), F32),
    gout=((12, 4, WIN, 128), F32),
    gdown=((12, 160, 128), F32),
    gact=((6, 16, WIN, 128), F32),
    pgrad=((4, 6, 128, 128), F32),
)


class Comm:
    def __init__(self):
        rows, dp = lax.axis_index("rows"), lax.axis_index("dp")
        self.rows, self.dp = rows, dp
        self.pos = {"z": rows // NX, "x": rows % NX, "y": dp // 2}
        self.core = dp % 2

    def device(self, **moved):
        at = {**self.pos, "core": self.core, **moved}
        return (at["z"] * NX + at["x"], at["y"] * 2 + at["core"])

    def greet(self):
        barrier = pltpu.get_barrier_semaphore()

        def one(k, _):
            peer = (lax.rem(self.rows + k, NROWS), self.dp)
            pl.semaphore_signal(barrier, inc=1, device_id=peer, device_id_type=MESH)
            return 0

        lax.fori_loop(1, NROWS, one, 0)
        for k in range(1, NDP):
            peer = (self.rows, lax.rem(self.dp + k, NDP))
            pl.semaphore_signal(barrier, inc=1, device_id=peer, device_id_type=MESH)

    def met(self):
        pl.semaphore_wait(pltpu.get_barrier_semaphore(), NROWS + NDP - 2)


def remote(src, dst, sems, k, device):
    return pltpu.make_async_remote_copy(
        src_ref=src,
        dst_ref=dst,
        send_sem=sems[0].at[k],
        recv_sem=sems[1].at[k],
        device_id=device,
        device_id_type=MESH,
    )


def wait_all(copies):
    for copy in copies:
        copy.wait()


def regroup_quad(c, r):
    quad, m = c.dp // 4 * 4, c.dp % 4
    copies = []
    for k in range(1, 4):
        other = lax.rem(m + k, 4)
        copy = remote(r.wpart.at[other], r.wquad.at[m], r.quad_sems, k, (c.rows, quad + other))
        copy.start()
        copies.append(copy)
    r.wquad[m] = r.wpart[m]
    yield
    wait_all(copies)
    row, col = iotas(48, 64)
    pick = one_hot((col // 16 * 12 + col % 16 == row) & (col % 16 < 12))
    block = jnp.dot(pick, r.wquad[...].reshape(64, 384), preferred_element_type=F32).astype(BF16)
    y = c.pos["y"]
    for j in range(3):
        r.w[y % 2, c.core, c.pos["z"], c.pos["x"], y // 2, j] = block[j * 16 : j * 16 + 16]


def gather_part(c, r, part):
    sub, lane, lanes, order = PARTS[part]
    sems = (r.wsend.at[part], r.wrecv.at[part])
    sent = []

    def block(core, whole, cut=slice(None), **at):
        at = {**c.pos, **at}
        z = cut if "z" in whole else at["z"]
        x = at["x"] if "x" not in whole else slice(None) if "z" in whole else cut
        yl, yh = (slice(None), slice(None)) if "y" in whole else (at["y"] % 2, at["y"] // 2)
        return r.w.at[yl, core, z, x, yh, sub, :, pl.ds(lane, lanes)]

    def push(mine, device):
        copy = remote(mine, mine, sems, len(sent), device)
        copy.start()
        sent.append(copy)
        return len(sent) - 1

    def arrived(k, got):
        remote(got, got, sems, k, c.device(core=1 - c.core)).wait_recv()

    for level in range(2):
        axis, whole = order[level], order[:level]
        n, here = SIZE[axis], c.pos[axis]
        slots = [
            push(block(c.core, whole), c.device(**{axis: lax.rem(here + k, n)})) for k in range(1, n)
        ]
        yield
        for k, slot in enumerate(slots):
            arrived(slot, block(c.core, whole, **{axis: lax.rem(here + n - 1 - k, n)}))
    axis, whole = order[2], order[:2]
    here, n = c.pos[axis], SIZE[axis]
    way = 1 - 2 * c.core
    sibling = c.device(core=1 - c.core)
    half = (NZ if "z" in whole else NX) // 2
    cuts = [pl.ds(0, half), pl.ds(half, half)]
    family = []

    def at(step):
        return {axis: lax.rem(here + step + 2 * n, n)}

    def mine(step, cut):
        return block(c.core, whole, cut, **at(step))

    def send(step, ahead, cut):
        return push(mine(step, cut), c.device(**at(ahead)))

    def share(step, cut):
        family.append((push(mine(step, cut), sibling), -step, cut))

    moving = {}
    for k, cut in enumerate(cuts):
        moving[k] = (send(0, way, cut), send(0, -way, cut))
    for cut in cuts:
        share(0, cut)
    for step in range(1, n // 2 + 1):
        for k, cut in enumerate(cuts):
            yield
            if step == n // 2:
                arrived(moving[k], mine(step, cut))
                family.append((push(mine(step, cut), sibling), step, cut))
                continue
            ahead, back = moving[k]
            arrived(ahead, mine(-way * step, cut))
            if step == n // 2 - 1:
                moving[k] = send(-way * step, way, cut)
            else:
                again = send(-way * step, way, cut)
            share(-way * step, cut)
            arrived(back, mine(way * step, cut))
            if step < n // 2 - 1:
                moving[k] = (again, send(way * step, -way, cut))
            share(way * step, cut)
    yield
    for slot, step, cut in family:
        arrived(slot, block(1 - c.core, whole, cut, **at(step)))
    for copy in sent:
        copy.wait_send()


def exchange_start(c, src, dst, sems):
    def one(turn, _):
        k = lax.rem(turn * 13, NROWS)
        peer = lax.rem(c.rows + k, NROWS)
        remote(
            src.at[pl.ds(peer * 16, 16)], dst.at[pl.ds(c.rows * 16, 16)], sems, k, (peer, c.dp)
        ).start()
        return 0

    lax.fori_loop(1, NROWS, one, 0)
    mine = pl.ds(pl.multiple_of(c.rows * 16, 16), 16)
    dst[mine] = src[mine]


def exchange_wait(c, src, dst, sems):
    def one(k, _):
        peer = lax.rem(c.rows - k + NROWS, NROWS)
        remote(
            src.at[pl.ds(peer * 16, 16)], dst.at[pl.ds(peer * 16, 16)], sems, k, (peer, c.dp)
        ).wait()
        return 0

    lax.fori_loop(1, NROWS, one, 0)


def to_all(n, here, src_of, dst, sems, device_of):
    copies = []
    for k in range(1, n):
        other = lax.rem(here + k, n)
        copy = remote(src_of(other), dst.at[here], sems, k, device_of(other))
        copy.start()
        copies.append(copy)
    return copies


def neighbours(c):
    return (
        (lax.rem(c.rows + NROWS - 1, NROWS), c.dp),
        (lax.rem(c.rows + 1, NROWS), c.dp),
    )


def pixel_halo(c, r):
    left, right = neighbours(c)
    copies = [
        remote(r.pix.at[pl.ds(0, 80)], r.pix_right.at[pl.ds(0, 80)], r.pix_sems, 0, left),
        remote(r.pix.at[pl.ds(432, 80)], r.pix_left.at[pl.ds(48, 80)], r.pix_sems, 1, right),
    ]
    for copy in copies:
        copy.start()
    r.pix_left[0:48] = jnp.zeros((48, 768), BF16)
    r.pix_right[80:128] = jnp.zeros((48, 768), BF16)
    return copies


def pack_cotangent(r):
    row, _ = iotas(512, 256)
    total = jnp.zeros((512, 768), F32)
    for half in range(2):
        pick = one_hot(row == r.own_row[...] + half)
        lines = r.cot[:, :, half * 768 : half * 768 + 768].astype(F32).reshape(256, 768)
        total = total + jnp.dot(pick, lines.astype(BF16), preferred_element_type=F32)
    r.cot_send[...] = total.astype(BF16)


def bring_cotangent(c, r):
    x = c.pos["x"]
    exchange_start(c, r.cot_send, r.cot_recv, r.cot_sems)
    yield
    exchange_wait(c, r.cot_send, r.cot_recv, r.cot_sems)
    _, col = iotas(256, 512)
    pick = one_hot(col == r.strip_col[...])
    lines = jnp.dot(pick, r.cot_recv[...], preferred_element_type=F32).astype(BF16)
    r.cot_mid[...] = lines.reshape(4, 64, 768)
    copies = to_all(
        NX, x, lambda o: r.cot_mid.at[o], r.cot_own, r.line_sems, lambda o: c.device(x=o)
    )
    r.cot_own[x] = r.cot_mid[x]
    yield
    wait_all(copies)
    left, right = neighbours(c)
    copies = [
        remote(r.cot_own.at[:, pl.ds(0, 16)], r.cot_right, r.edge_sems, 0, left),
        remote(r.cot_own.at[:, pl.ds(48, 16)], r.cot_left, r.edge_sems, 1, right),
    ]
    for copy in copies:
        copy.start()
    yield
    wait_all(copies)


def take_features(c, r):
    x = c.pos["x"]
    copies = to_all(
        NX, x, lambda o: r.feat_out.at[o], r.feat_mid, r.out_sems, lambda o: c.device(x=o)
    )
    r.feat_mid[x] = r.feat_out[x]
    yield
    wait_all(copies)
    row, _ = iotas(512, 256)
    pick = one_hot(row == r.strip_row[...])
    r.feat_send[...] = jnp.dot(
        pick, r.feat_mid[...].reshape(256, 768), preferred_element_type=F32
    ).astype(BF16)
    exchange_start(c, r.feat_send, r.feat_recv, r.feat_sems)
    yield
    exchange_wait(c, r.feat_send, r.feat_recv, r.feat_sems)
    _, col = iotas(256, 512)
    for half in range(2):
        pick = one_hot(col == r.own_col[...] + half)
        lines = jnp.dot(pick, r.feat_recv[...], preferred_element_type=F32)
        r.features[:, :, half * 768 : half * 768 + 768] = lines.reshape(64, 4, 768).astype(BF16)


def total_of(ref, n):
    total = ref[0]
    for k in range(1, n):
        total = total + ref[k]
    return total


def reduce_sums(c, r, which):
    sums, red_a, red_b, red_c, out, sems = (
        getattr(r, name + which) for name in ("sums", "red_a", "red_b", "red_c", "total", "sems")
    )
    x, z = c.pos["x"], c.pos["z"]
    size = sums.shape[0] // NDP
    split = red_b.shape[1] < size

    def family(k):
        return (sems[0].at[k], sems[1].at[k])

    def dp_device(other):
        return (c.rows, other)

    def x_device(other):
        return c.device(x=other)

    blocks = sums.reshape(NDP, size, 128)
    copies = to_all(NDP, c.dp, lambda o: blocks.at[o], red_a, family(0), dp_device)
    red_a[c.dp] = sums[pl.ds(pl.multiple_of(c.dp * size, 8), size), :]
    yield
    wait_all(copies)
    if split:
        r.part3[...] = total_of(red_a, NDP).reshape(NX, size // NX, 128)
        copies = to_all(NX, x, lambda o: r.part3.at[o], red_b, family(1), x_device)
        red_b[x] = r.part3[x]
    else:
        red_b[x] = total_of(red_a, NDP)
        copies = to_all(NX, x, lambda o: red_b.at[x], red_b, family(1), x_device)
    yield
    wait_all(copies)
    red_c[z] = total_of(red_b, NX)
    copies = to_all(NZ, z, lambda o: red_c.at[z], red_c, family(2), lambda o: c.device(z=o))
    yield
    wait_all(copies)
    if split:
        r.whole3[x] = total_of(red_c, NZ)
        copies = to_all(NX, x, lambda o: r.whole3.at[x], r.whole3, family(4), x_device)
        yield
        wait_all(copies)
        out[c.dp] = r.whole3[...].reshape(size, 128)
    else:
        out[c.dp] = total_of(red_c, NZ)
    copies = to_all(NDP, c.dp, lambda o: out.at[c.dp], out, family(3), dp_device)
    yield
    wait_all(copies)


class Drive:
    def __init__(self, *tasks):
        self.tasks = list(tasks)

    def step(self):
        for task in list(self.tasks):
            if next(task, "end") == "end":
                self.tasks.remove(task)

    def finish(self):
        while self.tasks:
            self.step()


COMM_SCRATCH = dict(
    w=((2, 2, NZ, NX, 2, 3, 16, 384), BF16),
    wpart=((4, 16, 384), BF16),
    wquad=((4, 16, 384), BF16),
    pix_left=((128, 768), BF16),
    pix_right=((128, 768), BF16),
    cot_send=((NROWS * 16, 768), BF16),
    cot_recv=((NROWS * 16, 768), BF16),
    cot_mid=((4, 64, 768), BF16),
    cot_own=((4, 64, 768), BF16),
    cot_left=((4, 16, 768), BF16),
    cot_right=((4, 16, 768), BF16),
    feat_out=((4, 64, 768), BF16),
    feat_mid=((4, 64, 768), BF16),
    feat_send=((NROWS * 16, 768), BF16),
    feat_recv=((NROWS * 16, 768), BF16),
    sums2=((NDP * ROWS_TWO, 128), F32),
    red_a2=((NDP, ROWS_TWO, 128), F32),
    red_b2=((NX, ROWS_TWO, 128), F32),
    red_c2=((NZ, ROWS_TWO, 128), F32),
    sums3=((NDP * ROWS_THREE, 128), F32),
    red_a3=((NDP, ROWS_THREE, 128), F32),
    part3=((NX, ROWS_THREE // NX, 128), F32),
    red_b3=((NX, ROWS_THREE // NX, 128), F32),
    red_c3=((NZ, ROWS_THREE // NX, 128), F32),
    whole3=((NX, ROWS_THREE // NX, 128), F32),
)
PAIRS = dict(
    quad_sems=(4,),
    pix_sems=(2,),
    cot_sems=(NROWS,),
    line_sems=(NX,),
    edge_sems=(2,),
    out_sems=(NX,),
    feat_sems=(NROWS,),
    sems2=(5, NDP),
    sems3=(5, NDP),
)
INPUTS = (
    "pix", "k2", "b2", "gain", "k3", "b3", "db", "weight", "cot", "heights", "widths", "owners"
)
OUTPUTS = ("features", "pixel_grad", "total2", "total3")


def whole_kernel(*refs):
    names = INPUTS + OUTPUTS + tuple(COMPUTE_SCRATCH) + tuple(COMM_SCRATCH)
    r = SimpleNamespace(**dict(zip(names, refs)))
    rest = refs[len(names) :]
    for k, name in enumerate(PAIRS):
        setattr(r, name, (rest[2 * k], rest[2 * k + 1]))
    r.wsend, r.wrecv = rest[2 * len(PAIRS) :]

    c = Comm()
    c.greet()
    load_weights(r)
    c.met()
    quad = regroup_quad(c, r)
    next(quad)
    halo = pixel_halo(c, r)
    make_tables(c, r)
    next(quad, None)
    weights = Drive(*[gather_part(c, r, part) for part in range(len(PARTS))])
    weights.step()
    load_parameters(r)
    spread_taps(r)
    for group in range(4):
        load_pixels(r, r.pix[group * 128 : group * 128 + 128, :], group + 1)
    pack_cotangent(r)
    wait_all(halo)
    load_pixels(r, r.pix_left[...], 0)
    load_pixels(r, r.pix_right[...], 5)
    weights.step()
    cot = Drive(bring_cotangent(c, r))
    cot.step()
    r.sums2[...] = jnp.zeros((NDP * ROWS_TWO, 128), F32)
    r.sums3[...] = jnp.zeros((NDP * ROWS_THREE, 128), F32)
    for ch in range(6):
        forward_two(r, ch)
        if ch == 4:
            weights.step()
    norm_two(r, 0, 16)
    weights.step()
    cot.step()
    weights.step()
    cot.step()
    weights.step()
    weights.step()
    cot.finish()
    place_cotangent(r)
    backward_three(r)
    weights.finish()
    for n in range(4):
        project(r, n)
    forward_three(r)
    pack_features(r)
    feat = Drive(take_features(c, r))
    feat.step()
    kernel_three(r, 0, 12)
    sums = Drive(reduce_sums(c, r, "3"))
    sums.step()
    project_back(r, 0)
    feat.step()
    for ab in range(1, 4):
        project_back(r, ab)
    norm_back(r)
    kernel_two(r, 0, 3)
    sums.step()
    kernel_two(r, 3, 6)
    last = Drive(reduce_sums(c, r, "2"))
    last.step()
    backward_two(r, 0, 4)
    sums.step()
    last.step()
    backward_two(r, 4, 6)
    store_pixel_grad(r)
    last.step()
    sums.step()
    feat.finish()
    last.step()
    sums.step()
    last.finish()
    sums.finish()


def run_kernel(*arrays):
    vmem = pl.BlockSpec(memory_space=pltpu.VMEM)
    scratch = [pltpu.VMEM(*v) for v in COMPUTE_SCRATCH.values()]
    scratch += [pltpu.VMEM(*v) for v in COMM_SCRATCH.values()]
    for shape in PAIRS.values():
        scratch += [pltpu.SemaphoreType.DMA(shape)] * 2
    scratch += [pltpu.SemaphoreType.DMA((len(PARTS), 40))] * 2
    return pl.pallas_call(
        whole_kernel,
        out_shape=(
            jax.ShapeDtypeStruct((64, 4, 1536), BF16),
            jax.ShapeDtypeStruct((512, 768), BF16),
            jax.ShapeDtypeStruct((NDP, ROWS_TWO, 128), F32),
            jax.ShapeDtypeStruct((NDP, ROWS_THREE, 128), F32),
        ),
        in_specs=[vmem] * len(INPUTS),
        out_specs=(vmem,) * 4,
        scratch_shapes=scratch,
        compiler_params=pltpu.CompilerParams(
            collective_id=0, has_side_effects=True, vmem_limit_bytes=60 * 1024 * 1024
        ),
    )(*arrays)


def body(
    pixels,
    kernel_two,
    bias_two,
    gain_two,
    down_weight,
    down_bias,
    kernel_three,
    bias_three,
    cotangent,
    tile_height,
    tile_width,
    tile_owner,
):
    features, pixel_grad, total2, total3 = run_kernel(
        pixels.reshape(512, 768),
        kernel_two,
        bias_two,
        gain_two,
        kernel_three,
        bias_three,
        down_bias,
        down_weight,
        cotangent[0],
        tile_height,
        tile_width,
        tile_owner,
    )
    factor = 1.0 / math.sqrt(NROWS * NDP * 64 * 8)
    two = total2.reshape(NDP * ROWS_TWO, 128)[:306].reshape(6, 51, 128) * factor
    two = two.transpose(1, 0, 2).reshape(51, 768)
    three = total3.reshape(NDP * ROWS_THREE, 128)[:600].reshape(12, 50, 128) * factor
    three = three.transpose(1, 0, 2).reshape(50, 1536)
    return (
        features.reshape(1, 64, 4, 1536),
        pixel_grad.reshape(1, 64, 8, 768),
        two[:49],
        two[49],
        two[50],
        three[:49],
        three[49],
    )


def solution(mesh):
    in_specs = (
        P("dp", "rows", None, None),
        P(),
        P(),
        P(),
        P(("rows", "dp"), None),
        P(),
        P(),
        P(),
        P("dp", "rows", None, None),
        P("dp", None),
        P("dp", None),
        P("dp", None),
    )
    out_specs = (P("dp", "rows", None, None), P("dp", "rows", None, None), P(), P(), P(), P(), P())
    return jax.shard_map(body, mesh=mesh, in_specs=in_specs, out_specs=out_specs, check_vma=False)
```
